512 devices in a mesh: dp: 4 (over x_hi, core), tp: 4 (over y), ep: 32 (over x_lo, z).
Axes of the slice: x: 4 (x_hi: 2, x_lo: 2; x = x_hi * 2 + x_lo), y: 4, z: 16, core: 2. Of those that a mesh axis runs over, the one named last changes fastest.
Arguments:
- queries: bfloat16 [384, 128, 576], P(('dp', 'ep'), 'tp'), may hold values from -24 to 24
- cache: bfloat16 [3072, 128, 576], P(('dp', 'tp', 'ep')), may hold values from -12 to 12
- tables: int32 [512, 6], P(('dp', 'tp', 'ep')), may hold values from 0 to 5, each once within a row
- lengths: int32 [4, 32, 3], P('dp', 'ep'), may hold values from 1 to 1024, 2048 in all within a row
- mig_cache: bfloat16 [1024, 128, 576], P(('dp', 'tp', 'ep')), may hold values from -12 to 12
- mig_src: int32 [32], P('ep'), may hold values from 0 to 3
- mig_dst: int32 [32], P('ep'), may hold values from 0 to 3, as said below
- mig_seq: int32 [32], P('ep'), may hold values from 0 to 2
- tokens: bfloat16 [8192, 3584], P(('dp', 'tp', 'ep')), may hold values from -6 to 6
- routes: int32 [8192, 2], P(('dp', 'tp', 'ep')), may hold values from 0 to 31, all different within a row; in each aligned block of 16 rows (0 to 15, 16 to 31, ...) at most 2 rows name the same one
- gates: float32 [8192, 2], P(('dp', 'tp', 'ep')), may hold values from 0.1 to 1
- gate_w: bfloat16 [32, 3584, 2048], P('ep', None, ('dp', 'tp')), may hold values from -0.09375 to 0.09375
- up_w: bfloat16 [32, 3584, 2048], P('ep', None, ('dp', 'tp')), may hold values from -0.09375 to 0.09375
- down_w: bfloat16 [32, 2048, 3584], P('ep', None, ('dp', 'tp')), may hold values from -0.125 to 0.125
Outputs:
- attn_out: bfloat16 [384, 128, 512], P(('dp', 'ep'), 'tp')
- moe_out: bfloat16 [8192, 3584], P(('dp', 'tp', 'ep'))
The draws below stay inside these ranges and needn't reach their ends.
Inputs may be any that keep to these rules, and one draw needn't show every extreme that they name: `tables`: each device's row is an ordering of its 6 page ids. The lengths of each group's 3 requests sum to 2048. `mig_dst`: differs from mig_src at every index. `routes`: each row names 2 different experts; in the rows of one device no expert is named more than 2 times, a bound that some block reaches.
All inputs are finite; a program needn't handle non-finite values.
Results may differ from the reference program's by a relative error of at most 0.0058.
Values may be sent and summed in bfloat16 or wider, within the bound.
No kernel may reach another device: no remote copies, remote signals or barrier semaphores. Data moves between devices by JAX's collectives and lax.ppermute only.
A program may use at most 64 MiB of HBM per device.

```python
import math
import jax
import jax.numpy as jnp
import numpy as np
from jax import lax

D = 3584
FF_E = 2048
HEADS = 128
KV_RANK = 512
ROPE_DIM = 64
PAGE = 128
SLOTS = 2
SEQS_G = 3
TOK_DEV = 16
TOP_WIN = 2
PAGES_DEV = 6
MAXLEN = 1024
CAP = 2
N_DP = 4
N_TP = 4
N_EP = 32
DEVICES = 512


def normal_rows(key, count):
    values = jax.random.normal(key, (count, PAGE, KV_RANK + ROPE_DIM), jnp.float32)
    return jnp.clip(values, -4.0, 4.0)


def migration_pair(key):
    source = jax.random.randint(jax.random.fold_in(key, 91), (N_EP,), 0, N_DP, dtype=jnp.int32)
    offset = jax.random.randint(jax.random.fold_in(key, 92), (N_EP,), 1, N_DP, dtype=jnp.int32)
    return (source, (source + offset) % N_DP)


def draw_queries(key, part):
    key = jax.random.fold_in(key, 17)
    key_main = jax.random.fold_in(key, 1)
    count = N_DP * N_EP * SEQS_G
    values = jnp.clip(jax.random.normal(key_main, (count, HEADS, KV_RANK + ROPE_DIM), jnp.float32), -4.0, 4.0)
    return values.astype(jnp.bfloat16)


def draw_cache(key, part):
    key = jax.random.fold_in(key, 21)
    values = normal_rows(jax.random.fold_in(key, 5), DEVICES * PAGES_DEV)
    return values.astype(jnp.bfloat16)


def draw_mig_cache(key, part):
    key = jax.random.fold_in(key, 23)
    values = normal_rows(jax.random.fold_in(key, 5), DEVICES * SLOTS)
    return values.astype(jnp.bfloat16)


def draw_mig_src(key, part):
    source, target = migration_pair(key)
    return source


def draw_mig_dst(key, part):
    source, target = migration_pair(key)
    return target


def plant(entries, own_key, low, high):
    spot = [jax.random.randint(jax.random.fold_in(own_key, axis), (), 0, length) for axis, length in enumerate(entries.shape)]
    longest = entries.shape.index(max(entries.shape))
    next_to = spot[:longest] + [(spot[longest] + 1) % entries.shape[longest]] + spot[longest + 1:]
    return entries.at[tuple(spot)].set(low).at[tuple(next_to)].set(high)


def block_scale(key, extent, cuts, smallest, high):
    def one(position, blocks):
        heights = jax.random.uniform(jax.random.fold_in(jax.random.fold_in(key, 6), position), (blocks,), jnp.float32, smallest / len(cuts), high / len(cuts))
        return jnp.repeat(jnp.exp(heights), extent[position] // blocks).reshape((-1,) + (1,) * (len(extent) - position - 1))

    factor_of = one(*cuts[0])
    for cut in cuts[1:]:
        factor_of = factor_of * one(*cut)
    return factor_of


def profile(amount, total, bound, slope):
    portions = [(1 << 20) // math.isqrt(grade ** slope) + 1 for grade in range(2, amount + 1)]
    spare, holding = total - bound - (amount - 1), [1] * (amount - 1)
    while spare > 0:
        free = [i for i in range(amount - 1) if holding[i] < bound]
        mass, remaining = sum([portions[i] for i in free]), spare
        for i in free:
            more = min(bound - holding[i], max(1, remaining * portions[i] // mass), spare)
            holding[i] = holding[i] + more
            spare = spare - more
    return np.array([bound] + holding)


def ragged_sizes(rng, count, total, reach, slope):
    if count == 2:
        one = jax.random.randint(rng, (), max(1, total - reach), min(reach, total - 1) + 1)
        return jnp.stack([one, total - one])
    sizes = jnp.asarray(profile(count, total, reach, slope), jnp.int32)
    couples = (count - 1) // 2
    source_of, receiver = sizes[1:1 + 2 * couples:2], sizes[2:2 + 2 * couples:2]
    margin = jnp.minimum(source_of - 1, reach - receiver)
    moved = jax.random.randint(jax.random.fold_in(rng, 1), (couples,), 0, 1 << 20) % (margin + 1)
    sizes = sizes.at[1:1 + 2 * couples:2].set(source_of - moved).at[2:2 + 2 * couples:2].set(receiver + moved)
    return sizes[jax.random.permutation(jax.random.fold_in(rng, 2), count)]


def shared_out(rng, own, number, rows, number_of, top, most, skew):
    sequence = jax.random.permutation(rng, number_of)
    crowded, ordinary = shares(number_of, rows * top, most, skew, True), shares(number_of, rows * top, most, skew, False)
    places = jnp.arange(number_of)

    def named(sizes, turn):
        used = int((sizes > 0).sum())
        fixed = max(1, used // 4)
        passed = fixed + (places - fixed + turn * (used - fixed)) % max(1, number_of - fixed)
        return jnp.zeros((number_of,), jnp.int32).at[sequence[jnp.where(places < fixed, places, passed)]].set(jnp.asarray(sizes, jnp.int32))

    sizes = jnp.where(number % 4 == 0, named(crowded, number // 4), named(ordinary, number - number // 4 - 1))
    mixed = jax.random.permutation(jax.random.fold_in(own, 3), number_of)
    source_of, receiver = mixed[0:number_of // 2 * 2:2], mixed[1:number_of // 2 * 2:2]
    margin = jnp.minimum(sizes[source_of] - 1, most - sizes[receiver]) // 2
    margin = jnp.where((source_of == sequence[0]) | (receiver == sequence[0]) | (sizes[receiver] == 0), 0, jnp.maximum(margin, 0))
    passed = jax.random.randint(jax.random.fold_in(own, 4), (number_of // 2,), 0, 1 << 20) % (margin + 1)
    sizes = sizes.at[source_of].add(-passed).at[receiver].add(passed)
    items = jnp.searchsorted(jnp.cumsum(sizes), jnp.arange(rows * top), side="right").astype(jnp.int32)
    listing = items.reshape(top, rows).T
    listing = listing[jax.random.permutation(jax.random.fold_in(own, 1), rows)]
    turn = jax.random.randint(jax.random.fold_in(own, 2), (rows, 1), 0, top)
    return jnp.take_along_axis(listing, (jnp.arange(top)[None, :] + turn) % top, axis=1)


def shares(amount, total, reach, lean, full):
    portions = [(1 << 20) // math.isqrt(rank ** lean) + 1 for rank in range(1, amount + 1)]
    largest = reach if full else min(reach, max(-(-total // amount), total * portions[0] // sum(portions)))
    least = 1 if total - largest >= amount - 1 else 0
    counts, rest = [largest] + [least] * (amount - 1), total - largest - least * (amount - 1)
    while rest > 0:
        candidates = [i for i in range(1, amount) if counts[i] < largest] or [i for i in range(1, amount) if counts[i] < reach]
        whole, left = sum([portions[i] for i in candidates]), rest
        for i in candidates:
            extra = min(reach - counts[i], max(1, left * portions[i] // whole), rest)
            counts[i] = counts[i] + extra
            rest = rest - extra
    return np.array(counts)


def bell_draw(rng, extent, scale, reach, pieces=(), kind=jnp.bfloat16):
    entries = jax.random.normal(rng, extent, jnp.float32) * scale
    if len(pieces) > 0:
        entries = block_scale(rng, extent, pieces, -0.22, 0.18) * entries
    return jnp.clip(entries, min=-reach, max=reach).astype(kind)


def setup_inputs(seed: int = 0) -> dict:
    splits = jax.random.split(jax.random.key(seed), 15)
    queries = draw_queries(jax.random.fold_in(splits[14], 71), 0)
    cache = draw_cache(jax.random.fold_in(splits[14], 71), 0)
    tables = jax.vmap(lambda own: jax.random.permutation(own, PAGES_DEV))(jax.random.split(splits[2], (N_DP * N_TP * N_EP))).reshape((N_DP * N_TP * N_EP, PAGES_DEV)).astype(jnp.int32)
    lengths = jax.vmap(lambda own: ragged_sizes(own, SEQS_G, 2 * MAXLEN, MAXLEN, 2))(jax.random.split(splits[3], N_DP * N_EP)).reshape((N_DP, N_EP, SEQS_G)).astype(jnp.int32)
    mig_cache = draw_mig_cache(jax.random.fold_in(splits[14], 71), 0)
    mig_src = draw_mig_src(jax.random.fold_in(splits[14], 71), 0)
    mig_dst = draw_mig_dst(jax.random.fold_in(splits[14], 71), 0)
    mig_seq = plant(jax.random.randint(splits[7], (N_EP,), 0, SEQS_G), jax.random.fold_in(splits[7], 1), 0, SEQS_G - 1).astype(jnp.int32)
    tokens = bell_draw(splits[8], (N_DP * N_TP * N_EP * TOK_DEV, D), 1.0, 6.0, ((0, 512),))
    routes_keys = jax.random.split(jax.random.fold_in(splits[9], 1), (N_DP * N_TP * N_EP * TOK_DEV) // TOK_DEV)
    routes_turns = jax.random.permutation(jax.random.fold_in(splits[9], 3), (N_DP * N_TP * N_EP * TOK_DEV) // TOK_DEV)
    routes = jax.vmap(lambda own, number: shared_out(jax.random.fold_in(splits[9], 2), own, number, TOK_DEV, N_EP, TOP_WIN, CAP, 2))(routes_keys, routes_turns).reshape((N_DP * N_TP * N_EP * TOK_DEV, TOP_WIN))
    gates = jnp.clip(jnp.exp(math.log(1.0) - 2.3025851 * jax.random.uniform(splits[10], (N_DP * N_TP * N_EP * TOK_DEV, TOP_WIN), jnp.float32) ** block_scale(splits[10], (N_DP * N_TP * N_EP * TOK_DEV, TOP_WIN), ((0, 512),), -0.2, 0.2)), 0.1, 1.0)
    gate_w = bell_draw(splits[11], (N_EP, D, FF_E), D ** -0.5, 0.09375, ((0, 32), (2, 16)))
    up_w = bell_draw(splits[12], (N_EP, D, FF_E), D ** -0.5, 0.09375, ((0, 32), (2, 16)))
    down_w = bell_draw(splits[13], (N_EP, FF_E, D), FF_E ** -0.5, 0.125, ((0, 32), (2, 16)))
    return {"queries": queries, "cache": cache, "tables": tables, "lengths": lengths, "mig_cache": mig_cache, "mig_src": mig_src, "mig_dst": mig_dst, "mig_seq": mig_seq, "tokens": tokens, "routes": routes, "gates": gates, "gate_w": gate_w, "up_w": up_w, "down_w": down_w}


score_scale = 0.07216878364870322
neg_fill = -1.0e30


def group_attention(query_group, key_parts, valid):
    scores = jnp.einsum('shc,tskc->tshk', query_group.astype(jnp.float32), key_parts.astype(jnp.float32)) * score_scale
    masked = jnp.where(valid[:, :, None, :], scores, neg_fill)
    part_max = jnp.max(masked, axis=3)
    weights = jnp.where(valid[:, :, None, :], jnp.exp(masked - part_max[..., None]), 0.0).astype(jnp.bfloat16)
    part_sum = jnp.sum(weights.astype(jnp.float32), axis=3)
    part_acc = jnp.einsum('tshk,tskc->tshc', weights.astype(jnp.float32), key_parts[..., :KV_RANK].astype(jnp.float32))
    most = jnp.max(part_max, axis=0)
    factor = jnp.exp(part_max - most)
    numerator = jnp.sum(part_acc * factor[..., None], axis=0)
    denominator = jnp.sum(part_sum * factor, axis=0)
    return (numerator / denominator[..., None]).astype(jnp.bfloat16)


def route_places(route_ids):
    flattened_index_list = route_ids.reshape(-1)
    matches = (flattened_index_list[:, None] == jnp.arange(N_EP)[None, :]).astype(jnp.int32)
    before = jnp.cumsum(matches, axis=0) - matches
    column = flattened_index_list * CAP + jnp.sum(before * matches, axis=1)
    return (column[:, None] == jnp.arange(N_EP * CAP)[None, :]).reshape(TOK_DEV, TOP_WIN, N_EP * CAP)


def reference(queries, cache, tables, lengths, mig_cache, mig_src, mig_dst, mig_seq, tokens, routes, gates, gate_w, up_w, down_w):
    row_width = KV_RANK + ROPE_DIM
    query_blocks = queries.reshape(N_DP, N_EP, SEQS_G, HEADS, row_width)
    page_pools = cache.reshape(N_DP, N_TP, N_EP, PAGES_DEV, PAGE, row_width)
    table_blocks = tables.reshape(N_DP, N_TP, N_EP, SEQS_G, SLOTS)
    moved_pages = mig_cache.reshape(N_DP, N_TP, N_EP, SLOTS, PAGE, row_width)
    positions = ((jnp.arange(SLOTS)[None, :, None] * N_TP + jnp.arange(N_TP)[:, None, None]) * PAGE
                 + jnp.arange(PAGE)[None, None, :]).reshape(N_TP, SLOTS * PAGE)

    def one_group(index):
        dp_index = index // N_EP
        ep_index = index % N_EP
        query_group = query_blocks[dp_index, ep_index]
        pools = page_pools[dp_index, :, ep_index]
        picks = table_blocks[dp_index, :, ep_index]
        own_pages = jax.vmap(lambda page_pool, page_index_list: page_pool[page_index_list])(pools, picks)
        incoming = moved_pages[mig_src[ep_index], :, ep_index]
        chosen = (dp_index == mig_dst[ep_index]) & (jnp.arange(SEQS_G) == mig_seq[ep_index])
        key_parts = jnp.where(chosen[None, :, None, None, None], incoming[:, None], own_pages)
        key_parts = key_parts.reshape(N_TP, SEQS_G, SLOTS * PAGE, row_width)
        valid = positions[:, None, :] < lengths[dp_index, ep_index][None, :, None]
        return group_attention(query_group, key_parts, valid)

    grouped = lax.map(one_group, jnp.arange(N_DP * N_EP))
    attn_out = grouped.reshape(N_DP * N_EP * SEQS_G, HEADS, KV_RANK)

    devices_all = N_DP * N_TP * N_EP
    width = tokens.shape[1]
    places = jax.vmap(route_places)(routes.reshape(devices_all, TOK_DEV, TOP_WIN))
    selected_entries = jnp.any(places, axis=2).astype(jnp.float32)
    token_block_table = tokens.reshape(devices_all, TOK_DEV, width)
    dispatched_rows = jnp.einsum('cit,cip->ctp', selected_entries, token_block_table.astype(jnp.float32)).astype(jnp.bfloat16)
    expert_rows = dispatched_rows.reshape(devices_all, N_EP, CAP, width).transpose(1, 0, 2, 3).reshape(N_EP, devices_all * CAP, width)

    def one_expert(operands):
        rows_in, weight_gate, weight_up, weight_down = operands
        rows_wide = rows_in.astype(jnp.float32)
        gate = jnp.dot(rows_wide, weight_gate.astype(jnp.float32), preferred_element_type=jnp.float32)
        upward = jnp.dot(rows_wide, weight_up.astype(jnp.float32), preferred_element_type=jnp.float32)
        hidden = (jax.nn.silu(gate) * upward).astype(jnp.bfloat16)
        return jnp.dot(hidden.astype(jnp.float32), weight_down.astype(jnp.float32), preferred_element_type=jnp.float32).astype(jnp.bfloat16)

    expert_out = lax.map(one_expert, (expert_rows, gate_w, up_w, down_w))
    returned = expert_out.reshape(N_EP, devices_all, CAP, width).transpose(1, 0, 2, 3).reshape(devices_all, N_EP * CAP, width)
    chosen_rows = jnp.einsum('drkm,dmf->drkf', places.astype(jnp.float32), returned.astype(jnp.float32))
    mixed = jnp.sum(chosen_rows * gates.reshape(devices_all, TOK_DEV, TOP_WIN)[..., None], axis=2)
    moe_out = mixed.reshape(devices_all * TOK_DEV, width).astype(jnp.bfloat16)
    return (attn_out, moe_out)
```

```python
import jax
import jax.numpy as jnp
from jax import lax
from jax.experimental import pallas as pl
from jax.experimental.pallas import tpu as pltpu
from jax.sharding import PartitionSpec as P

KV_RANK = 512
ROPE_DIM = 64
PAGE = 128
SLOTS = 2
ROW = KV_RANK + ROPE_DIM
WIDE = 640
CAP = 2
N_TP = 4
N_DP = 4

score_scale = 0.07216878364870322
neg_fill = -1e30
f32 = jnp.float32
bf16 = jnp.bfloat16

VMEM = pl.BlockSpec(memory_space=pltpu.VMEM)
SMEM = pl.BlockSpec(memory_space=pltpu.SMEM)
ANY = pl.BlockSpec(memory_space=pl.ANY)


def params(mib):
    return pltpu.CompilerParams(vmem_limit_bytes=mib << 20)


def iota(shape, dim):
    return lax.broadcasted_iota(jnp.int32, shape, dim)


def route_slots(routes_ref):
    n = routes_ref.shape[1]
    sub, lane = iota((n, n), 0), iota((n, n), 1)
    rows = [routes_ref[k : k + 1, :].astype(f32) for k in range(2)]
    cols = [jnp.sum(jnp.where(sub == lane, r, 0.0), axis=1, keepdims=True) for r in rows]
    slot_rows, slot_cols = [], []
    for k in range(2):
        hits = jnp.where(cols[0] == rows[k], 1.0, 0.0) + jnp.where(cols[1] == rows[k], 1.0, 0.0)
        count = jnp.sum(jnp.where(sub < lane, hits, 0.0), axis=0, keepdims=True)
        slot_rows.append(rows[k] * CAP + count)
        hits = jnp.where(rows[0] == cols[k], 1.0, 0.0) + jnp.where(rows[1] == cols[k], 1.0, 0.0)
        count = jnp.sum(jnp.where(lane < sub, hits, 0.0), axis=1, keepdims=True)
        slot_cols.append(cols[k] * CAP + count)
    return slot_rows, slot_cols


def dispatch_kernel(routes_ref, tok_ref, out_ref):
    slot_rows, _ = route_slots(routes_ref)
    rows, quarter = out_ref.shape
    n = tok_ref.shape[0]
    place = iota((rows, n), 0)
    total = jnp.zeros((rows, quarter), f32)
    for q in range(4):
        t0 = slot_rows[0].astype(jnp.int32) * 4 + q
        t1 = slot_rows[1].astype(jnp.int32) * 4 + q
        pick = jnp.where((place == t0) | (place == t1), 1.0, 0.0).astype(bf16)
        total += jnp.dot(
            pick, tok_ref[:, q * quarter : (q + 1) * quarter], preferred_element_type=f32
        )
    out_ref[...] = total.astype(bf16)


def hidden_kernel(
    where_ref, b0, b1, b2, b3, w0, w1, w2, w3, out_ref, rows_ref, weights, sems
):
    rank_dp, rank_tp = where_ref[0], where_ref[1]
    depth, part = w0.shape[0] // 2, w0.shape[1]
    copies = []
    for rel, w in enumerate((w0, w1, w2, w3)):
        slot = rank_dp ^ rel
        for half in range(2):
            copy = pltpu.make_async_copy(
                w.at[pl.ds(half * depth, depth), :],
                weights.at[slot, :, pl.ds(half * part, part)],
                sems.at[rel, half],
            )
            copy.start()
            copies.append(copy)
    count, quarter = b0.shape
    slots = count // 4
    for k, b in enumerate((b0, b1, b2, b3)):
        base = pl.multiple_of(((rank_tp + N_TP - k) % N_TP) * slots, slots)
        block = b[...]
        for q in range(4):
            pick = jnp.where(
                iota((slots, count), 1) == iota((slots, count), 0) * 4 + q, 1.0, 0.0
            ).astype(bf16)
            rows_ref[pl.ds(base, slots), q * quarter : (q + 1) * quarter] = jnp.dot(
                pick, block, preferred_element_type=f32
            ).astype(bf16)
    for copy in copies:
        copy.wait()
    for i in range(N_DP):
        both = jnp.dot(rows_ref[...], weights[i], preferred_element_type=f32)
        gate, up = both[:, :part], both[:, part:]
        hidden = gate / (1.0 + jnp.exp(-gate)) * up
        out_ref[:, i * part : (i + 1) * part] = hidden.astype(bf16)


def down_kernel(where_ref, h0, h1, h2, h3, d0, d1, d2, d3, out_ref, hidden, weights, sems):
    rank_dp, rank_tp = where_ref[0], where_ref[1]
    cols = d0.shape[0]
    part = h0.shape[1] // N_DP
    copies = []
    for rel, d in enumerate((d0, d1, d2, d3)):
        base = pl.multiple_of((rank_dp ^ rel) * cols, 16)
        copy = pltpu.make_async_copy(d, weights.at[pl.ds(base, cols), :], sems.at[rel])
        copy.start()
        copies.append(copy)
    for k, h in enumerate((h0, h1, h2, h3)):
        source = (rank_tp + N_TP - k) % N_TP
        for i in range(N_DP):
            base = pl.multiple_of((i * N_TP + source) * part, part)
            hidden[:, pl.ds(base, part)] = h[:, i * part : (i + 1) * part]
    for copy in copies:
        copy.wait()
    out_ref[...] = lax.dot_general(
        hidden[...], weights[...], (((1,), (1,)), ((), ())), preferred_element_type=f32
    ).astype(bf16)


def combine_kernel(routes_ref, gates_ref, back_ref, out_ref):
    _, slot_cols = route_slots(routes_ref)
    n = out_ref.shape[0]
    slots = back_ref.shape[0] // N_TP
    part = back_ref.shape[1] // N_DP
    eye = iota((n, n), 0) == iota((n, n), 1)
    lane = iota((n, slots), 1)
    picks, gates = [], []
    for k in range(2):
        picks.append(
            jnp.where(lane == slot_cols[k].astype(jnp.int32), 1.0, 0.0).astype(bf16)
        )
        gates.append(
            jnp.sum(jnp.where(eye, gates_ref[k : k + 1, :], 0.0), axis=1, keepdims=True)
        )
    pieces = [None] * (N_TP * N_DP)
    for t in range(N_TP):
        block = back_ref[t * slots : (t + 1) * slots, :]
        mixed = gates[0] * jnp.dot(picks[0], block, preferred_element_type=f32) + gates[
            1
        ] * jnp.dot(picks[1], block, preferred_element_type=f32)
        for i in range(N_DP):
            pieces[i * N_TP + t] = mixed[:, i * part : (i + 1) * part]
    out_ref[...] = jnp.concatenate(pieces, axis=1).astype(bf16)


def split3(x):
    hi = x.astype(bf16)
    rest = x - hi.astype(f32)
    mid = rest.astype(bf16)
    low = (rest - mid.astype(f32)).astype(bf16)
    return hi, mid, low


def attend_kernel(
    where_ref, tables_ref, lengths_ref, q0, q1, q2, q3, cache, mig, o0, o1, o2, o3
):
    rank_tp = where_ref[1]
    heads = q0.shape[0] // 4
    for s in range(4):
        query = jnp.concatenate(
            [q[s * heads : (s + 1) * heads, :] for q in (q0, q1, q2, q3)], axis=0
        )
        total_heads = query.shape[0]
        if s < 3:
            length = lengths_ref[s].astype(f32)
        else:
            length = query[:, ROW : ROW + 1].astype(f32) * 256.0 + query[
                :, ROW + 1 : ROW + 2
            ].astype(f32)
        query = query[:, :ROW]
        keys, scores, valid = [], [], []
        for j in range(SLOTS):
            keys.append(cache[tables_ref[s * SLOTS + j]] if s < 3 else mig[j])
            score = jnp.dot(query, keys[j], preferred_element_type=f32) * score_scale
            place = ((j * N_TP + rank_tp) * PAGE + iota(score.shape, 1)).astype(f32)
            valid.append(place < length)
            scores.append(jnp.where(valid[j], score, neg_fill))
        top = jnp.max(jnp.maximum(scores[0], scores[1]), axis=1, keepdims=True)
        total = jnp.zeros((total_heads, 1), f32)
        acc = jnp.zeros((total_heads, KV_RANK), f32)
        for j in range(SLOTS):
            weight = jnp.where(valid[j], jnp.exp(scores[j] - top), 0.0).astype(bf16)
            total += jnp.sum(weight.astype(f32), axis=1, keepdims=True)
            acc += lax.dot_general(
                weight, keys[j][:KV_RANK, :], (((1,), (1,)), ((), ())), preferred_element_type=f32
            )
        some = total > 0.0
        safe = jnp.where(some, total, 1.0)
        mean = (acc / safe).astype(bf16)
        level = jnp.where(some, top + jnp.log(safe), neg_fill)
        hi, mid, low = split3(level)
        lane = iota((total_heads, WIDE - KV_RANK), 1)
        tail = jnp.where(
            lane == 0,
            hi.astype(f32),
            jnp.where(lane == 1, mid.astype(f32), jnp.where(lane == 2, low.astype(f32), 0.0)),
        ).astype(bf16)
        for k, o in enumerate((o0, o1, o2, o3)):
            o[s * heads : (s + 1) * heads, :KV_RANK] = mean[k * heads : (k + 1) * heads]
            o[s * heads : (s + 1) * heads, KV_RANK:] = tail[k * heads : (k + 1) * heads]


def merge_kernel(p0, p1, p2, p3, out_ref):
    levels = []
    for p in (p0, p1, p2, p3):
        tail = p[:, KV_RANK:].astype(f32)
        levels.append(tail[:, 0:1] + tail[:, 1:2] + tail[:, 2:3])
    most = jnp.maximum(jnp.maximum(levels[0], levels[1]), jnp.maximum(levels[2], levels[3]))
    numerator = jnp.zeros(out_ref.shape, f32)
    denominator = jnp.zeros((out_ref.shape[0], 1), f32)
    for p, level in zip((p0, p1, p2, p3), levels):
        factor = jnp.exp(level - most)
        denominator += factor
        numerator += factor * p[:, :KV_RANK].astype(f32)
    out_ref[...] = (numerator / denominator).astype(bf16)


def shift(x, k):
    return lax.ppermute(x, "tp", [(i, (i + k) % N_TP) for i in range(N_TP)])


def swap(x, bit):
    return lax.ppermute(x, "dp", [(i, i ^ bit) for i in range(N_DP)])


def per_device(
    queries,
    cache,
    tables,
    lengths,
    mig_cache,
    mig_src,
    mig_dst,
    mig_seq,
    tokens,
    routes,
    gates,
    gate_w,
    up_w,
    down_w,
):
    rank_tp = lax.axis_index("tp")
    rank_dp = lax.axis_index("dp")
    where = jnp.stack([rank_dp, rank_tp]).astype(jnp.int32)
    ranks_ep = lax.axis_size("ep")
    token_rows, width = tokens.shape
    slots_all = ranks_ep * CAP
    quarter = width // 4
    routes_t = routes.T
    gates_t = gates.T

    sent = pl.pallas_call(
        dispatch_kernel,
        out_shape=jax.ShapeDtypeStruct((slots_all * 4, quarter), bf16),
        in_specs=[VMEM] * 2,
        out_specs=VMEM,
        compiler_params=params(24),
    )(routes_t, tokens)
    arrived = lax.all_to_all(
        sent.reshape(ranks_ep, CAP * 4, quarter), "ep", split_axis=0, concat_axis=0, tiled=True
    ).reshape(slots_all * 4, quarter)

    first = jnp.concatenate([gate_w[0], up_w[0]], axis=0)
    first_x = swap(first, 2)
    first_c = swap(first, 1)
    first_xc = swap(first_x, 1)
    second = down_w[0].T
    second_c = swap(second, 1)

    heads = queries.shape[1]
    at_dst = rank_dp == mig_dst[0]
    picked = lax.dynamic_index_in_dim(queries, mig_seq[0], 0, keepdims=False)
    picked_len = lax.dynamic_index_in_dim(lengths[0, 0], mig_seq[0], 0, keepdims=False)
    lane = jnp.arange(WIDE - ROW)[None, :]
    tail = jnp.where(
        lane == 0, picked_len // 256, jnp.where(lane == 1, picked_len % 256, 0)
    ).astype(bf16)
    moving = jnp.concatenate([picked, jnp.broadcast_to(tail, (heads, WIDE - ROW))], axis=1)
    moving = jnp.where(at_dst, moving, jnp.zeros_like(moving))
    moving = moving + swap(moving, 1)
    moving = moving + swap(moving, 2)
    own = jnp.pad(queries.reshape(3 * heads, ROW), ((0, 0), (0, WIDE - ROW)))
    asked = jnp.concatenate([own, moving], axis=0)
    asks = [asked] + [shift(asked, k) for k in (1, 2, 3)]
    parts = pl.pallas_call(
        attend_kernel,
        out_shape=[jax.ShapeDtypeStruct((4 * heads, WIDE), bf16)] * 4,
        in_specs=[SMEM] * 3 + [VMEM] * 6,
        out_specs=[VMEM] * 4,
        compiler_params=params(32),
    )(
        where,
        tables.reshape(-1),
        lengths.reshape(-1),
        *asks,
        jnp.swapaxes(cache, 1, 2),
        jnp.swapaxes(mig_cache, 1, 2),
    )
    merged = pl.pallas_call(
        merge_kernel,
        out_shape=jax.ShapeDtypeStruct((4 * heads, KV_RANK), bf16),
        in_specs=[VMEM] * 4,
        out_specs=VMEM,
        compiler_params=params(16),
    )(parts[0], *[shift(parts[k], -k) for k in (1, 2, 3)])
    back = merged[3 * heads :]
    back = jnp.where(rank_dp == mig_src[0], back, jnp.zeros_like(back))
    back = back + swap(back, 1)
    back = back + swap(back, 2)
    chosen = at_dst & (jnp.arange(3) == mig_seq[0])
    attn_out = jnp.where(
        chosen[:, None, None], back[None], merged[: 3 * heads].reshape(3, heads, KV_RANK)
    )

    arrived, second_late = lax.optimization_barrier((arrived, second))
    second_x = swap(second_late, 2)
    second_xc = swap(second_x, 1)
    blocks = [arrived] + [shift(arrived, k) for k in (1, 2, 3)]
    part = gate_w.shape[2]
    rows = N_TP * slots_all
    hidden = pl.pallas_call(
        hidden_kernel,
        out_shape=jax.ShapeDtypeStruct((rows, N_DP * part), bf16),
        in_specs=[SMEM] + [VMEM] * 4 + [ANY] * 4,
        out_specs=VMEM,
        scratch_shapes=[
            pltpu.VMEM((rows, width), bf16),
            pltpu.VMEM((N_DP, width, 2 * part), bf16),
            pltpu.SemaphoreType.DMA((N_DP, 2)),
        ],
        compiler_params=params(40),
    )(where, *blocks, first, first_c, first_x, first_xc)
    hiddens = [hidden] + [shift(hidden, k) for k in (1, 2, 3)]
    cols = second.shape[0]
    expert_out = pl.pallas_call(
        down_kernel,
        out_shape=jax.ShapeDtypeStruct((rows, N_DP * cols), bf16),
        in_specs=[SMEM] + [VMEM] * 4 + [ANY] * 4,
        out_specs=VMEM,
        scratch_shapes=[
            pltpu.VMEM((rows, second.shape[1]), bf16),
            pltpu.VMEM((N_DP * cols, second.shape[1]), bf16),
            pltpu.SemaphoreType.DMA((N_DP,)),
        ],
        compiler_params=params(32),
    )(where, *hiddens, second, second_c, second_x, second_xc)
    returned = lax.all_to_all(
        expert_out.reshape(N_TP * ranks_ep, CAP, N_DP * cols),
        ("tp", "ep"),
        split_axis=0,
        concat_axis=0,
        tiled=True,
    ).reshape(rows, N_DP * cols)
    moe_out = pl.pallas_call(
        combine_kernel,
        out_shape=jax.ShapeDtypeStruct((token_rows, width), bf16),
        in_specs=[VMEM] * 3,
        out_specs=VMEM,
        compiler_params=params(16),
    )(routes_t, gates_t, returned)
    return (attn_out, moe_out)


def solution(mesh):
    in_specs = (
        P(("dp", "ep"), "tp", None),
        P(("dp", "tp", "ep"), None, None),
        P(("dp", "tp", "ep"), None),
        P("dp", "ep", None),
        P(("dp", "tp", "ep"), None, None),
        P("ep"),
        P("ep"),
        P("ep"),
        P(("dp", "tp", "ep"), None),
        P(("dp", "tp", "ep"), None),
        P(("dp", "tp", "ep"), None),
        P("ep", None, ("dp", "tp")),
        P("ep", None, ("dp", "tp")),
        P("ep", None, ("dp", "tp")),
    )
    out_specs = (P(("dp", "ep"), "tp", None), P(("dp", "tp", "ep"), None))
    return jax.shard_map(
        per_device, mesh=mesh, in_specs=in_specs, out_specs=out_specs, check_vma=False
    )
```

```python
import jax
import jax.numpy as jnp
from jax import lax
from jax.experimental import pallas as pl
from jax.experimental.pallas import tpu as pltpu
from jax.sharding import PartitionSpec as P

KV_RANK = 512
ROPE_DIM = 64
PAGE = 128
SLOTS = 2
ROW = KV_RANK + ROPE_DIM
WIDE = 640
CAP = 2
N_TP = 4
N_DP = 4

score_scale = 0.07216878364870322
neg_fill = -1e30
f32 = jnp.float32
bf16 = jnp.bfloat16

VMEM = pl.BlockSpec(memory_space=pltpu.VMEM)
SMEM = pl.BlockSpec(memory_space=pltpu.SMEM)
ANY = pl.BlockSpec(memory_space=pl.ANY)


def params(mib):
    return pltpu.CompilerParams(vmem_limit_bytes=mib << 20)


def iota(shape, dim):
    return lax.broadcasted_iota(jnp.int32, shape, dim)


def route_slots(routes_ref):
    n = routes_ref.shape[1]
    sub, lane = iota((n, n), 0), iota((n, n), 1)
    rows = [routes_ref[k : k + 1, :].astype(f32) for k in range(2)]
    cols = [jnp.sum(jnp.where(sub == lane, r, 0.0), axis=1, keepdims=True) for r in rows]
    slot_rows, slot_cols = [], []
    for k in range(2):
        hits = jnp.where(cols[0] == rows[k], 1.0, 0.0) + jnp.where(cols[1] == rows[k], 1.0, 0.0)
        count = jnp.sum(jnp.where(sub < lane, hits, 0.0), axis=0, keepdims=True)
        slot_rows.append(rows[k] * CAP + count)
        hits = jnp.where(rows[0] == cols[k], 1.0, 0.0) + jnp.where(rows[1] == cols[k], 1.0, 0.0)
        count = jnp.sum(jnp.where(lane < sub, hits, 0.0), axis=1, keepdims=True)
        slot_cols.append(cols[k] * CAP + count)
    return slot_rows, slot_cols


def dispatch_kernel(routes_ref, tok_ref, out_ref):
    slot_rows, _ = route_slots(routes_ref)
    rows, quarter = out_ref.shape
    n = tok_ref.shape[0]
    place = iota((rows, n), 0)
    total = jnp.zeros((rows, quarter), f32)
    for q in range(4):
        t0 = slot_rows[0].astype(jnp.int32) * 4 + q
        t1 = slot_rows[1].astype(jnp.int32) * 4 + q
        pick = jnp.where((place == t0) | (place == t1), 1.0, 0.0).astype(bf16)
        total += jnp.dot(
            pick, tok_ref[:, q * quarter : (q + 1) * quarter], preferred_element_type=f32
        )
    out_ref[...] = total.astype(bf16)


def hidden_kernel(
    where_ref, b0, b1, b2, b3, w0, w1, w2, w3, out_ref, rows_ref, weights, sems,
    held, block_sems,
):
    rank_dp, rank_tp = where_ref[0], where_ref[1]
    depth, part = w0.shape[0] // 2, w0.shape[1]
    landing = []
    for k, b in enumerate((b0, b1, b2, b3)):
        copy = pltpu.make_async_copy(b, held.at[k], block_sems.at[k])
        copy.start()
        landing.append(copy)
    copies = []
    for rel, w in enumerate((w0, w1, w2, w3)):
        slot = rank_dp ^ rel
        for half in range(2):
            copy = pltpu.make_async_copy(
                w.at[pl.ds(half * depth, depth), :],
                weights.at[slot, :, pl.ds(half * part, part)],
                sems.at[rel, half],
            )
            copy.start()
            copies.append(copy)
    count, quarter = b0.shape
    slots = count // 4
    for k in range(N_TP):
        base = pl.multiple_of(((rank_tp + N_TP - k) % N_TP) * slots, slots)
        landing[k].wait()
        block = held[k]
        for q in range(4):
            pick = jnp.where(
                iota((slots, count), 1) == iota((slots, count), 0) * 4 + q, 1.0, 0.0
            ).astype(bf16)
            rows_ref[pl.ds(base, slots), q * quarter : (q + 1) * quarter] = jnp.dot(
                pick, block, preferred_element_type=f32
            ).astype(bf16)
    for copy in copies:
        copy.wait()
    for i in range(N_DP):
        both = jnp.dot(rows_ref[...], weights[i], preferred_element_type=f32)
        gate, up = both[:, :part], both[:, part:]
        hidden = gate / (1.0 + jnp.exp(-gate)) * up
        out_ref[:, i * part : (i + 1) * part] = hidden.astype(bf16)


def down_kernel(where_ref, h0, h1, h2, h3, d0, d1, d2, d3, out_ref, hidden, weights, sems):
    rank_dp, rank_tp = where_ref[0], where_ref[1]
    cols = d0.shape[0]
    part = h0.shape[1] // N_DP
    copies = []
    for rel, d in enumerate((d0, d1, d2, d3)):
        base = pl.multiple_of((rank_dp ^ rel) * cols, 16)
        copy = pltpu.make_async_copy(d, weights.at[pl.ds(base, cols), :], sems.at[rel])
        copy.start()
        copies.append(copy)
    for k, h in enumerate((h0, h1, h2, h3)):
        source = (rank_tp + N_TP - k) % N_TP
        for i in range(N_DP):
            base = pl.multiple_of((i * N_TP + source) * part, part)
            hidden[:, pl.ds(base, part)] = h[:, i * part : (i + 1) * part]
    for copy in copies:
        copy.wait()
    out_ref[...] = lax.dot_general(
        hidden[...], weights[...], (((1,), (1,)), ((), ())), preferred_element_type=f32
    ).astype(bf16)


def combine_kernel(routes_ref, gates_ref, back_ref, out_ref):
    _, slot_cols = route_slots(routes_ref)
    n = out_ref.shape[0]
    slots = back_ref.shape[0] // N_TP
    part = back_ref.shape[1] // N_DP
    eye = iota((n, n), 0) == iota((n, n), 1)
    lane = iota((n, slots), 1)
    picks, gates = [], []
    for k in range(2):
        picks.append(
            jnp.where(lane == slot_cols[k].astype(jnp.int32), 1.0, 0.0).astype(bf16)
        )
        gates.append(
            jnp.sum(jnp.where(eye, gates_ref[k : k + 1, :], 0.0), axis=1, keepdims=True)
        )
    pieces = [None] * (N_TP * N_DP)
    for t in range(N_TP):
        block = back_ref[t * slots : (t + 1) * slots, :]
        mixed = gates[0] * jnp.dot(picks[0], block, preferred_element_type=f32) + gates[
            1
        ] * jnp.dot(picks[1], block, preferred_element_type=f32)
        for i in range(N_DP):
            pieces[i * N_TP + t] = mixed[:, i * part : (i + 1) * part]
    out_ref[...] = jnp.concatenate(pieces, axis=1).astype(bf16)


def split3(x):
    hi = x.astype(bf16)
    rest = x - hi.astype(f32)
    mid = rest.astype(bf16)
    low = (rest - mid.astype(f32)).astype(bf16)
    return hi, mid, low


def attend_kernel(
    where_ref,
    tables_ref,
    lengths_ref,
    a0,
    a1,
    a2,
    a3,
    pool,
    m0,
    m1,
    m2,
    m3,
    o0,
    o1,
    o2,
    o3,
    pages,
    sem,
    asked,
    cache,
    sems,
):
    rank_dp, rank_tp = where_ref[0], where_ref[1]
    source, target, moved = where_ref[2], where_ref[3], where_ref[4]
    copies = [pltpu.make_async_copy(pool, cache, sems.at[N_TP])]
    for k, a in enumerate((a0, a1, a2, a3)):
        copies.append(pltpu.make_async_copy(a, asked.at[k], sems.at[k]))
    for copy in copies:
        copy.start()
    for rel, m in enumerate((m0, m1, m2, m3)):

        @pl.when(source == (rank_dp ^ rel))
        def _(m=m):
            copy = pltpu.make_async_copy(m, pages, sem)
            copy.start()
            copy.wait()

    for copy in copies:
        copy.wait()
    q0, q1, q2, q3 = [asked[k] for k in range(N_TP)]
    heads = q0.shape[0] // 3
    for s in range(3):
        query = jnp.concatenate(
            [q[s * heads : (s + 1) * heads, :] for q in (q0, q1, q2, q3)], axis=0
        )
        total_heads = query.shape[0]
        length = lengths_ref[s]
        use_moved = (rank_dp == target) & (moved == s)
        keys, scores, valid = [], [], []
        for j in range(SLOTS):
            own = cache[tables_ref[s * SLOTS + j]]
            keys.append(jnp.where(use_moved, pages[j * ROW : (j + 1) * ROW, :], own))
            score = jnp.dot(query, keys[j], preferred_element_type=f32) * score_scale
            place = (j * N_TP + rank_tp) * PAGE + iota(score.shape, 1)
            valid.append(place < length)
            scores.append(jnp.where(valid[j], score, neg_fill))
        top = jnp.max(jnp.maximum(scores[0], scores[1]), axis=1, keepdims=True)
        total = jnp.zeros((total_heads, 1), f32)
        acc = jnp.zeros((total_heads, KV_RANK), f32)
        for j in range(SLOTS):
            weight = jnp.where(valid[j], jnp.exp(scores[j] - top), 0.0).astype(bf16)
            total += jnp.sum(weight.astype(f32), axis=1, keepdims=True)
            acc += lax.dot_general(
                weight, keys[j][:KV_RANK, :], (((1,), (1,)), ((), ())), preferred_element_type=f32
            )
        some = total > 0.0
        safe = jnp.where(some, total, 1.0)
        mean = (acc / safe).astype(bf16)
        level = jnp.where(some, top + jnp.log(safe), neg_fill)
        hi, mid, low = split3(level)
        lane = iota((total_heads, WIDE - KV_RANK), 1)
        tail = jnp.where(
            lane == 0,
            hi.astype(f32),
            jnp.where(lane == 1, mid.astype(f32), jnp.where(lane == 2, low.astype(f32), 0.0)),
        ).astype(bf16)
        for k, o in enumerate((o0, o1, o2, o3)):
            o[s * heads : (s + 1) * heads, :KV_RANK] = mean[k * heads : (k + 1) * heads]
            o[s * heads : (s + 1) * heads, KV_RANK:] = tail[k * heads : (k + 1) * heads]


def merge_kernel(p0, p1, p2, p3, out_ref):
    levels = []
    for p in (p0, p1, p2, p3):
        tail = p[:, KV_RANK:].astype(f32)
        levels.append(tail[:, 0:1] + tail[:, 1:2] + tail[:, 2:3])
    most = jnp.maximum(jnp.maximum(levels[0], levels[1]), jnp.maximum(levels[2], levels[3]))
    numerator = jnp.zeros(out_ref.shape, f32)
    denominator = jnp.zeros((out_ref.shape[0], 1), f32)
    for p, level in zip((p0, p1, p2, p3), levels):
        factor = jnp.exp(level - most)
        denominator += factor
        numerator += factor * p[:, :KV_RANK].astype(f32)
    out_ref[...] = (numerator / denominator).astype(bf16)


def shift(x, k):
    return lax.ppermute(x, "tp", [(i, (i + k) % N_TP) for i in range(N_TP)])


def swap(x, bit):
    return lax.ppermute(x, "dp", [(i, i ^ bit) for i in range(N_DP)])


def per_device(
    queries,
    cache,
    tables,
    lengths,
    mig_cache,
    mig_src,
    mig_dst,
    mig_seq,
    tokens,
    routes,
    gates,
    gate_w,
    up_w,
    down_w,
):
    rank_tp = lax.axis_index("tp")
    rank_dp = lax.axis_index("dp")
    where = jnp.stack([rank_dp, rank_tp, mig_src[0], mig_dst[0], mig_seq[0]]).astype(jnp.int32)
    ranks_ep = lax.axis_size("ep")
    token_rows, width = tokens.shape
    slots_all = ranks_ep * CAP
    quarter = width // 4
    part = gate_w.shape[2]
    routes_t = routes.T
    gates_t = gates.T
    after = lax.optimization_barrier

    sent = pl.pallas_call(
        dispatch_kernel,
        out_shape=jax.ShapeDtypeStruct((slots_all * 4, quarter), bf16),
        in_specs=[VMEM] * 2,
        out_specs=VMEM,
        compiler_params=params(24),
    )(routes_t, tokens)
    arrived = lax.all_to_all(
        sent.reshape(ranks_ep, CAP * 4, quarter), "ep", split_axis=0, concat_axis=0, tiled=True
    ).reshape(slots_all * 4, quarter)

    gate, up, queries, down, pages, _ = after(
        (gate_w[0], up_w[0], queries, down_w[0].T, jnp.swapaxes(mig_cache, 1, 2), sent)
    )
    first = jnp.concatenate([gate, up], axis=0)
    first_x = swap(first, 2)
    first_c = swap(first, 1)
    down_c = swap(down, 1)
    pages = pages.reshape(-1, PAGE)
    pages_c = swap(pages, 1)
    heads = queries.shape[1]
    asked = queries.reshape(3 * heads, ROW)
    asks = [shift(asked, k) for k in (1, 2, 3)]
    arrived, first_c, down_c, where, *asks = after((arrived, first_c, down_c, where, *asks))

    blocks = [shift(arrived, k) for k in (1, 2, 3)]
    first_x, pages_c, *blocks = after((first_x, pages_c, *blocks))
    first_xc = swap(first_x, 1)
    down_x = swap(after((down, first_x))[0], 2)
    rows = N_TP * slots_all
    hidden = pl.pallas_call(
        hidden_kernel,
        out_shape=jax.ShapeDtypeStruct((rows, N_DP * part), bf16),
        in_specs=[SMEM] + [ANY] * 8,
        out_specs=VMEM,
        scratch_shapes=[
            pltpu.VMEM((rows, width), bf16),
            pltpu.VMEM((N_DP, width, 2 * part), bf16),
            pltpu.SemaphoreType.DMA((N_DP, 2)),
            pltpu.VMEM((N_TP,) + arrived.shape, bf16),
            pltpu.SemaphoreType.DMA((N_TP,)),
        ],
        compiler_params=params(58),
    )(where, arrived, *blocks, first, first_c, first_x, first_xc)
    pages_x = swap(after((pages, hidden))[0], 2)
    hiddens = [hidden] + [shift(hidden, k) for k in (1, 2, 3)]
    pages_x, *hiddens = after((pages_x, *hiddens))
    down_xc = swap(after((down_x, *hiddens))[0], 1)
    cols = down.shape[0]
    expert_out = pl.pallas_call(
        down_kernel,
        out_shape=jax.ShapeDtypeStruct((rows, N_DP * cols), bf16),
        in_specs=[SMEM] + [VMEM] * 4 + [ANY] * 4,
        out_specs=VMEM,
        scratch_shapes=[
            pltpu.VMEM((rows, down.shape[1]), bf16),
            pltpu.VMEM((N_DP * cols, down.shape[1]), bf16),
            pltpu.SemaphoreType.DMA((N_DP,)),
        ],
        compiler_params=params(32),
    )(where, *hiddens, down, down_c, down_x, down_xc)
    returned = lax.all_to_all(
        expert_out.reshape(N_TP * ranks_ep, CAP, N_DP * cols),
        ("tp", "ep"),
        split_axis=0,
        concat_axis=0,
        tiled=True,
    ).reshape(rows, N_DP * cols)

    pages_xc = swap(pages_x, 1)
    parts = pl.pallas_call(
        attend_kernel,
        out_shape=[jax.ShapeDtypeStruct((3 * heads, WIDE), bf16)] * 4,
        in_specs=[SMEM] * 3 + [ANY] * 9,
        out_specs=[VMEM] * 4,
        scratch_shapes=[
            pltpu.VMEM((SLOTS * ROW, PAGE), bf16),
            pltpu.SemaphoreType.DMA,
            pltpu.VMEM((N_TP,) + asked.shape, bf16),
            pltpu.VMEM((cache.shape[0], ROW, PAGE), bf16),
            pltpu.SemaphoreType.DMA((N_TP + 1,)),
        ],
        compiler_params=params(32),
    )(
        where,
        tables.reshape(-1),
        lengths.reshape(-1),
        asked,
        *asks,
        jnp.swapaxes(cache, 1, 2),
        pages,
        pages_c,
        pages_x,
        pages_xc,
    )
    merged = pl.pallas_call(
        merge_kernel,
        out_shape=jax.ShapeDtypeStruct((3 * heads, KV_RANK), bf16),
        in_specs=[VMEM] * 4,
        out_specs=VMEM,
        compiler_params=params(16),
    )(parts[0], *[shift(parts[k], -k) for k in (1, 2, 3)])
    attn_out = merged.reshape(3, heads, KV_RANK)
    moe_out = pl.pallas_call(
        combine_kernel,
        out_shape=jax.ShapeDtypeStruct((token_rows, width), bf16),
        in_specs=[VMEM] * 3,
        out_specs=VMEM,
        compiler_params=params(16),
    )(routes_t, gates_t, returned)
    return (attn_out, moe_out)


def solution(mesh):
    in_specs = (
        P(("dp", "ep"), "tp", None),
        P(("dp", "tp", "ep"), None, None),
        P(("dp", "tp", "ep"), None),
        P("dp", "ep", None),
        P(("dp", "tp", "ep"), None, None),
        P("ep"),
        P("ep"),
        P("ep"),
        P(("dp", "tp", "ep"), None),
        P(("dp", "tp", "ep"), None),
        P(("dp", "tp", "ep"), None),
        P("ep", None, ("dp", "tp")),
        P("ep", None, ("dp", "tp")),
        P("ep", None, ("dp", "tp")),
    )
    out_specs = (P(("dp", "ep"), "tp", None), P(("dp", "tp", "ep"), None))
    return jax.shard_map(
        per_device, mesh=mesh, in_specs=in_specs, out_specs=out_specs, check_vma=False
    )
```

```python
import jax
import jax.numpy as jnp
from jax import lax
from jax.experimental import pallas as pl
from jax.experimental.pallas import tpu as pltpu
from jax.sharding import PartitionSpec as P

KV_RANK = 512
ROPE_DIM = 64
PAGE = 128
SLOTS = 2
ROW = KV_RANK + ROPE_DIM
WIDE = 640
CAP = 2
N_TP = 4
N_DP = 4

score_scale = 0.07216878364870322
neg_fill = -1e30
f32 = jnp.float32
bf16 = jnp.bfloat16

VMEM = pl.BlockSpec(memory_space=pltpu.VMEM)
SMEM = pl.BlockSpec(memory_space=pltpu.SMEM)
ANY = pl.BlockSpec(memory_space=pl.ANY)


def params(mib):
    return pltpu.CompilerParams(vmem_limit_bytes=mib << 20)


def iota(shape, dim):
    return lax.broadcasted_iota(jnp.int32, shape, dim)


def route_slots(routes_ref):
    n = routes_ref.shape[1]
    sub, lane = iota((n, n), 0), iota((n, n), 1)
    rows = [routes_ref[k : k + 1, :].astype(f32) for k in range(2)]
    cols = [jnp.sum(jnp.where(sub == lane, r, 0.0), axis=1, keepdims=True) for r in rows]
    slot_rows, slot_cols = [], []
    for k in range(2):
        hits = jnp.where(cols[0] == rows[k], 1.0, 0.0) + jnp.where(cols[1] == rows[k], 1.0, 0.0)
        count = jnp.sum(jnp.where(sub < lane, hits, 0.0), axis=0, keepdims=True)
        slot_rows.append(rows[k] * CAP + count)
        hits = jnp.where(rows[0] == cols[k], 1.0, 0.0) + jnp.where(rows[1] == cols[k], 1.0, 0.0)
        count = jnp.sum(jnp.where(lane < sub, hits, 0.0), axis=1, keepdims=True)
        slot_cols.append(cols[k] * CAP + count)
    return slot_rows, slot_cols


def dispatch_kernel(routes_any, tok_any, out_ref, routes_ref, tok_ref, sems):
    copies = [
        pltpu.make_async_copy(routes_any, routes_ref, sems.at[0]),
        pltpu.make_async_copy(tok_any, tok_ref, sems.at[1]),
    ]
    for copy in copies:
        copy.start()
    for copy in copies:
        copy.wait()
    slot_rows, _ = route_slots(routes_ref)
    rows, quarter = out_ref.shape
    n = tok_ref.shape[0]
    place = iota((rows, n), 0)
    total = jnp.zeros((rows, quarter), f32)
    for q in range(4):
        t0 = slot_rows[0].astype(jnp.int32) * 4 + q
        t1 = slot_rows[1].astype(jnp.int32) * 4 + q
        pick = jnp.where((place == t0) | (place == t1), 1.0, 0.0).astype(bf16)
        total += jnp.dot(
            pick, tok_ref[:, q * quarter : (q + 1) * quarter], preferred_element_type=f32
        )
    out_ref[...] = total.astype(bf16)


def hidden_kernel(
    where_ref, b0, b1, b2, b3, w0, w1, w2, w3, out_ref, rows_ref, weights, sems,
    held, block_sems,
):
    rank_dp, rank_tp = where_ref[0], where_ref[1]
    depth, part = w0.shape[0] // 2, w0.shape[1]
    landing = []
    for k, b in enumerate((b0, b1, b2, b3)):
        copy = pltpu.make_async_copy(b, held.at[k], block_sems.at[k])
        copy.start()
        landing.append(copy)
    copies = []
    for rel, w in enumerate((w0, w1, w2, w3)):
        slot = rank_dp ^ rel
        for half in range(2):
            copy = pltpu.make_async_copy(
                w.at[pl.ds(half * depth, depth), :],
                weights.at[slot, :, pl.ds(half * part, part)],
                sems.at[rel, half],
            )
            copy.start()
            copies.append(copy)
    count, quarter = b0.shape
    slots = count // 4
    for k in range(N_TP):
        base = pl.multiple_of(((rank_tp + N_TP - k) % N_TP) * slots, slots)
        landing[k].wait()
        block = held[k]
        for q in range(4):
            pick = jnp.where(
                iota((slots, count), 1) == iota((slots, count), 0) * 4 + q, 1.0, 0.0
            ).astype(bf16)
            rows_ref[pl.ds(base, slots), q * quarter : (q + 1) * quarter] = jnp.dot(
                pick, block, preferred_element_type=f32
            ).astype(bf16)
    for copy in copies:
        copy.wait()
    for i in range(N_DP):
        both = jnp.dot(rows_ref[...], weights[i], preferred_element_type=f32)
        gate, up = both[:, :part], both[:, part:]
        hidden = gate / (1.0 + jnp.exp(-gate)) * up
        for copy in range(out_ref.shape[0]):
            out_ref[copy, :, i * part : (i + 1) * part] = hidden.astype(bf16)


def down_kernel(where_ref, parts, d0, d1, d2, d3, out_ref, hidden, weights, sems):
    rank_dp = where_ref[0]
    cols = d0.shape[0]
    part = parts.shape[2] // N_DP
    copies = []
    for rel, d in enumerate((d0, d1, d2, d3)):
        base = pl.multiple_of((rank_dp ^ rel) * cols, 16)
        copy = pltpu.make_async_copy(d, weights.at[pl.ds(base, cols), :], sems.at[rel])
        copy.start()
        copies.append(copy)
    for t in range(N_TP):
        for i in range(N_DP):
            base = (i * N_TP + t) * part
            hidden[:, base : base + part] = parts[t, :, i * part : (i + 1) * part]
    for copy in copies:
        copy.wait()
    out_ref[...] = lax.dot_general(
        hidden[...], weights[...], (((1,), (1,)), ((), ())), preferred_element_type=f32
    ).astype(bf16)


def combine_kernel(routes_ref, gates_ref, back_ref, out_ref):
    _, slot_cols = route_slots(routes_ref)
    n = out_ref.shape[0]
    slots = back_ref.shape[0] // N_TP
    part = back_ref.shape[1] // N_DP
    eye = iota((n, n), 0) == iota((n, n), 1)
    lane = iota((n, slots), 1)
    picks, gates = [], []
    for k in range(2):
        picks.append(
            jnp.where(lane == slot_cols[k].astype(jnp.int32), 1.0, 0.0).astype(bf16)
        )
        gates.append(
            jnp.sum(jnp.where(eye, gates_ref[k : k + 1, :], 0.0), axis=1, keepdims=True)
        )
    pieces = [None] * (N_TP * N_DP)
    for t in range(N_TP):
        block = back_ref[t * slots : (t + 1) * slots, :]
        mixed = gates[0] * jnp.dot(picks[0], block, preferred_element_type=f32) + gates[
            1
        ] * jnp.dot(picks[1], block, preferred_element_type=f32)
        for i in range(N_DP):
            pieces[i * N_TP + t] = mixed[:, i * part : (i + 1) * part]
    out_ref[...] = jnp.concatenate(pieces, axis=1).astype(bf16)


def split3(x):
    hi = x.astype(bf16)
    rest = x - hi.astype(f32)
    mid = rest.astype(bf16)
    low = (rest - mid.astype(f32)).astype(bf16)
    return hi, mid, low


def attend_kernel(
    where_ref,
    tables_ref,
    lengths_ref,
    a0,
    a1,
    far,
    pool,
    m0,
    m1,
    m2,
    m3,
    o0,
    o1,
    o2,
    o3,
    pages,
    sem,
    asked,
    cache,
    sems,
):
    rank_dp, rank_tp = where_ref[0], where_ref[1]
    source, target, moved = where_ref[2], where_ref[3], where_ref[4]
    copies = [pltpu.make_async_copy(pool, cache, sems.at[N_TP])]
    rows = a0.shape[0]
    pairs = (a0, a1, far.at[pl.ds(0, rows), :], far.at[pl.ds(rows, rows), :])
    for k, a in enumerate(pairs):
        copies.append(pltpu.make_async_copy(a, asked.at[k], sems.at[k]))
    for copy in copies:
        copy.start()
    for rel, m in enumerate((m0, m1, m2, m3)):

        @pl.when(source == (rank_dp ^ rel))
        def _(m=m):
            copy = pltpu.make_async_copy(m, pages, sem)
            copy.start()
            copy.wait()

    for copy in copies:
        copy.wait()
    q0, q1, q2, q3 = [asked[k] for k in range(N_TP)]
    heads = q0.shape[0] // 3
    for s in range(3):
        query = jnp.concatenate(
            [q[s * heads : (s + 1) * heads, :] for q in (q0, q1, q2, q3)], axis=0
        )
        total_heads = query.shape[0]
        length = lengths_ref[s]
        use_moved = (rank_dp == target) & (moved == s)
        keys, scores, valid = [], [], []
        for j in range(SLOTS):
            own = cache[tables_ref[s * SLOTS + j]]
            keys.append(jnp.where(use_moved, pages[j * ROW : (j + 1) * ROW, :], own))
            score = jnp.dot(query, keys[j], preferred_element_type=f32) * score_scale
            place = (j * N_TP + rank_tp) * PAGE + iota(score.shape, 1)
            valid.append(place < length)
            scores.append(jnp.where(valid[j], score, neg_fill))
        top = jnp.max(jnp.maximum(scores[0], scores[1]), axis=1, keepdims=True)
        total = jnp.zeros((total_heads, 1), f32)
        acc = jnp.zeros((total_heads, KV_RANK), f32)
        for j in range(SLOTS):
            weight = jnp.where(valid[j], jnp.exp(scores[j] - top), 0.0).astype(bf16)
            total += jnp.sum(weight.astype(f32), axis=1, keepdims=True)
            acc += lax.dot_general(
                weight, keys[j][:KV_RANK, :], (((1,), (1,)), ((), ())), preferred_element_type=f32
            )
        some = total > 0.0
        safe = jnp.where(some, total, 1.0)
        mean = (acc / safe).astype(bf16)
        level = jnp.where(some, top + jnp.log(safe), neg_fill)
        hi, mid, low = split3(level)
        lane = iota((total_heads, WIDE - KV_RANK), 1)
        tail = jnp.where(
            lane == 0,
            hi.astype(f32),
            jnp.where(lane == 1, mid.astype(f32), jnp.where(lane == 2, low.astype(f32), 0.0)),
        ).astype(bf16)
        for k, o in enumerate((o0, o1, o2, o3)):
            o[s * heads : (s + 1) * heads, :KV_RANK] = mean[k * heads : (k + 1) * heads]
            o[s * heads : (s + 1) * heads, KV_RANK:] = tail[k * heads : (k + 1) * heads]


def merge_kernel(p0, p1, p2, p3, out_ref):
    levels = []
    for p in (p0, p1, p2, p3):
        tail = p[:, KV_RANK:].astype(f32)
        levels.append(tail[:, 0:1] + tail[:, 1:2] + tail[:, 2:3])
    most = jnp.maximum(jnp.maximum(levels[0], levels[1]), jnp.maximum(levels[2], levels[3]))
    numerator = jnp.zeros(out_ref.shape, f32)
    denominator = jnp.zeros((out_ref.shape[0], 1), f32)
    for p, level in zip((p0, p1, p2, p3), levels):
        factor = jnp.exp(level - most)
        denominator += factor
        numerator += factor * p[:, :KV_RANK].astype(f32)
    out_ref[...] = (numerator / denominator).astype(bf16)


def shift(x, k):
    return lax.ppermute(x, "tp", [(i, (i + k) % N_TP) for i in range(N_TP)])


def swap(x, bit):
    return lax.ppermute(x, "dp", [(i, i ^ bit) for i in range(N_DP)])


def per_device(
    queries,
    cache,
    tables,
    lengths,
    mig_cache,
    mig_src,
    mig_dst,
    mig_seq,
    tokens,
    routes,
    gates,
    gate_w,
    up_w,
    down_w,
):
    rank_tp = lax.axis_index("tp")
    rank_dp = lax.axis_index("dp")
    where = jnp.stack([rank_dp, rank_tp, mig_src[0], mig_dst[0], mig_seq[0]]).astype(jnp.int32)
    ranks_ep = lax.axis_size("ep")
    token_rows, width = tokens.shape
    slots_all = ranks_ep * CAP
    quarter = width // 4
    part = gate_w.shape[2]
    routes_t = routes.T
    gates_t = gates.T
    after = lax.optimization_barrier

    sent = pl.pallas_call(
        dispatch_kernel,
        out_shape=jax.ShapeDtypeStruct((slots_all * 4, quarter), bf16),
        in_specs=[ANY] * 2,
        out_specs=VMEM,
        scratch_shapes=[
            pltpu.VMEM(routes_t.shape, routes_t.dtype),
            pltpu.VMEM(tokens.shape, tokens.dtype),
            pltpu.SemaphoreType.DMA((2,)),
        ],
        compiler_params=params(58),
    )(routes_t, tokens)
    arrived = lax.all_to_all(
        sent.reshape(ranks_ep, CAP * 4, quarter), "ep", split_axis=0, concat_axis=0, tiled=True
    ).reshape(slots_all * 4, quarter)

    gate, up, queries, down, pages, _ = after(
        (gate_w[0], up_w[0], queries, down_w[0].T, jnp.swapaxes(mig_cache, 1, 2), sent)
    )
    first = jnp.concatenate([gate, up], axis=0)
    first_x = swap(first, 2)
    first_c = swap(first, 1)
    down_c = swap(down, 1)
    pages = pages.reshape(-1, PAGE)
    heads = queries.shape[1]
    asked = queries.reshape(3 * heads, ROW)
    near = shift(asked, 1)
    far = shift(jnp.concatenate([asked, near], axis=0), 2)
    pages_c = swap(pages, 1)
    arrived, down_c, pages_c, where, near = after((arrived, down_c, pages_c, where, near))

    blocks = [shift(arrived, k) for k in (1, 2, 3)]
    first_x, first_c, far, *blocks = after((first_x, first_c, far, *blocks))
    asks = [near, far]
    first_xc = swap(first_x, 1)
    down_x = swap(after((down, first_x))[0], 2)
    rows = N_TP * slots_all
    hidden = pl.pallas_call(
        hidden_kernel,
        out_shape=jax.ShapeDtypeStruct((N_TP, rows, N_DP * part), bf16),
        in_specs=[SMEM] + [ANY] * 8,
        out_specs=VMEM,
        scratch_shapes=[
            pltpu.VMEM((rows, width), bf16),
            pltpu.VMEM((N_DP, width, 2 * part), bf16),
            pltpu.SemaphoreType.DMA((N_DP, 2)),
            pltpu.VMEM((N_TP,) + arrived.shape, bf16),
            pltpu.SemaphoreType.DMA((N_TP,)),
        ],
        compiler_params=params(58),
    )(where, arrived, *blocks, first, first_c, first_x, first_xc)
    pages_x = swap(after((pages, hidden))[0], 2)
    hiddens = [lax.all_to_all(hidden, "tp", split_axis=0, concat_axis=0, tiled=True)]
    pages_x, *hiddens = after((pages_x, *hiddens))
    down_xc = swap(after((down_x, *hiddens))[0], 1)
    cols = down.shape[0]
    expert_out = pl.pallas_call(
        down_kernel,
        out_shape=jax.ShapeDtypeStruct((rows, N_DP * cols), bf16),
        in_specs=[SMEM] + [VMEM] + [ANY] * 4,
        out_specs=VMEM,
        scratch_shapes=[
            pltpu.VMEM((rows, down.shape[1]), bf16),
            pltpu.VMEM((N_DP * cols, down.shape[1]), bf16),
            pltpu.SemaphoreType.DMA((N_DP,)),
        ],
        compiler_params=params(32),
    )(where, *hiddens, down, down_c, down_x, down_xc)
    returned = lax.all_to_all(
        expert_out.reshape(N_TP * ranks_ep, CAP, N_DP * cols),
        ("tp", "ep"),
        split_axis=0,
        concat_axis=0,
        tiled=True,
    ).reshape(rows, N_DP * cols)

    pages_xc = swap(pages_x, 1)
    parts = pl.pallas_call(
        attend_kernel,
        out_shape=[jax.ShapeDtypeStruct((3 * heads, WIDE), bf16)] * 4,
        in_specs=[SMEM] * 3 + [ANY] * 8,
        out_specs=[VMEM] * 4,
        scratch_shapes=[
            pltpu.VMEM((SLOTS * ROW, PAGE), bf16),
            pltpu.SemaphoreType.DMA,
            pltpu.VMEM((N_TP,) + asked.shape, bf16),
            pltpu.VMEM((cache.shape[0], ROW, PAGE), bf16),
            pltpu.SemaphoreType.DMA((N_TP + 1,)),
        ],
        compiler_params=params(32),
    )(
        where,
        tables.reshape(-1),
        lengths.reshape(-1),
        asked,
        *asks,
        jnp.swapaxes(cache, 1, 2),
        pages,
        pages_c,
        pages_x,
        pages_xc,
    )
    merged = pl.pallas_call(
        merge_kernel,
        out_shape=jax.ShapeDtypeStruct((3 * heads, KV_RANK), bf16),
        in_specs=[VMEM] * 4,
        out_specs=VMEM,
        compiler_params=params(16),
    )(parts[0], *[shift(parts[k], -k) for k in (1, 2, 3)])
    attn_out = merged.reshape(3, heads, KV_RANK)
    moe_out = pl.pallas_call(
        combine_kernel,
        out_shape=jax.ShapeDtypeStruct((token_rows, width), bf16),
        in_specs=[VMEM] * 3,
        out_specs=VMEM,
        compiler_params=params(16),
    )(routes_t, gates_t, returned)
    return (attn_out, moe_out)


def solution(mesh):
    in_specs = (
        P(("dp", "ep"), "tp", None),
        P(("dp", "tp", "ep"), None, None),
        P(("dp", "tp", "ep"), None),
        P("dp", "ep", None),
        P(("dp", "tp", "ep"), None, None),
        P("ep"),
        P("ep"),
        P("ep"),
        P(("dp", "tp", "ep"), None),
        P(("dp", "tp", "ep"), None),
        P(("dp", "tp", "ep"), None),
        P("ep", None, ("dp", "tp")),
        P("ep", None, ("dp", "tp")),
        P("ep", None, ("dp", "tp")),
    )
    out_specs = (P(("dp", "ep"), "tp", None), P(("dp", "tp", "ep"), None))
    return jax.shard_map(
        per_device, mesh=mesh, in_specs=in_specs, out_specs=out_specs, check_vma=False
    )
```

```python
import jax
import jax.numpy as jnp
from jax import lax
from jax.experimental import pallas as pl
from jax.experimental.pallas import tpu as pltpu
from jax.sharding import PartitionSpec as P

KV_RANK = 512
ROPE_DIM = 64
PAGE = 128
SLOTS = 2
ROW = KV_RANK + ROPE_DIM
WIDE = 640
CAP = 2
N_TP = 4
N_DP = 4

score_scale = 0.07216878364870322
neg_fill = -1e30
f32 = jnp.float32
bf16 = jnp.bfloat16

VMEM = pl.BlockSpec(memory_space=pltpu.VMEM)
SMEM = pl.BlockSpec(memory_space=pltpu.SMEM)
ANY = pl.BlockSpec(memory_space=pl.ANY)


def params(mib):
    return pltpu.CompilerParams(vmem_limit_bytes=mib << 20)


def iota(shape, dim):
    return lax.broadcasted_iota(jnp.int32, shape, dim)


def route_slots(routes_ref):
    n = routes_ref.shape[1]
    sub, lane = iota((n, n), 0), iota((n, n), 1)
    rows = [routes_ref[k : k + 1, :].astype(f32) for k in range(2)]
    cols = [jnp.sum(jnp.where(sub == lane, r, 0.0), axis=1, keepdims=True) for r in rows]
    slot_rows, slot_cols = [], []
    for k in range(2):
        hits = jnp.where(cols[0] == rows[k], 1.0, 0.0) + jnp.where(cols[1] == rows[k], 1.0, 0.0)
        count = jnp.sum(jnp.where(sub < lane, hits, 0.0), axis=0, keepdims=True)
        slot_rows.append(rows[k] * CAP + count)
        hits = jnp.where(rows[0] == cols[k], 1.0, 0.0) + jnp.where(rows[1] == cols[k], 1.0, 0.0)
        count = jnp.sum(jnp.where(lane < sub, hits, 0.0), axis=1, keepdims=True)
        slot_cols.append(cols[k] * CAP + count)
    return slot_rows, slot_cols


def dispatch_kernel(routes_any, tok_any, out_ref, routes_ref, tok_ref, sems):
    copies = [
        pltpu.make_async_copy(routes_any, routes_ref, sems.at[0]),
        pltpu.make_async_copy(tok_any, tok_ref, sems.at[1]),
    ]
    for copy in copies:
        copy.start()
    for copy in copies:
        copy.wait()
    slot_rows, _ = route_slots(routes_ref)
    rows, quarter = out_ref.shape
    n = tok_ref.shape[0]
    place = iota((rows, n), 0)
    total = jnp.zeros((rows, quarter), f32)
    for q in range(4):
        t0 = slot_rows[0].astype(jnp.int32) * 4 + q
        t1 = slot_rows[1].astype(jnp.int32) * 4 + q
        pick = jnp.where((place == t0) | (place == t1), 1.0, 0.0).astype(bf16)
        total += jnp.dot(
            pick, tok_ref[:, q * quarter : (q + 1) * quarter], preferred_element_type=f32
        )
    out_ref[...] = total.astype(bf16)


def hidden_kernel(where_ref, b0, b1, b2, b3, w0, w1, w2, w3, out_ref, rows_ref):
    rank_dp, rank_tp = where_ref[0], where_ref[1]
    depth, part = w0.shape[0] // 2, w0.shape[1]
    count, quarter = b0.shape
    slots = count // 4
    for k, b in enumerate((b0, b1, b2, b3)):
        base = pl.multiple_of(((rank_tp + N_TP - k) % N_TP) * slots, slots)
        block = b[...]
        row = iota((count, count), 0)
        pick = jnp.where(
            iota((count, count), 1) == (row % slots) * 4 + row // slots, 1.0, 0.0
        ).astype(bf16)
        sorted_rows = jnp.dot(pick, block, preferred_element_type=f32).astype(bf16)
        for q in range(4):
            rows_ref[pl.ds(base, slots), q * quarter : (q + 1) * quarter] = sorted_rows[
                q * slots : (q + 1) * slots
            ]
    for rel, w in enumerate((w0, w1, w2, w3)):
        both = jnp.dot(
            rows_ref[...],
            jnp.concatenate([w[:depth, :], w[depth:, :]], axis=1),
            preferred_element_type=f32,
        )
        gate, up = both[:, :part], both[:, part:]
        hidden = (gate / (1.0 + jnp.exp(-gate)) * up).astype(bf16)
        base = pl.multiple_of((rank_dp ^ rel) * part, part)
        for copy in range(out_ref.shape[0]):
            out_ref[copy, :, pl.ds(base, part)] = hidden


def down_kernel(where_ref, parts, d0, d1, d2, d3, out_ref, hidden, weights, sems):
    rank_dp = where_ref[0]
    cols = d0.shape[0]
    part = parts.shape[2] // N_DP
    copies = []
    for rel, d in enumerate((d0, d1, d2, d3)):
        base = pl.multiple_of((rank_dp ^ rel) * cols, 16)
        copy = pltpu.make_async_copy(d, weights.at[pl.ds(base, cols), :], sems.at[rel])
        copy.start()
        copies.append(copy)
    for t in range(N_TP):
        for i in range(N_DP):
            base = (i * N_TP + t) * part
            hidden[:, base : base + part] = parts[t, :, i * part : (i + 1) * part]
    for copy in copies:
        copy.wait()
    out_ref[...] = lax.dot_general(
        hidden[...], weights[...], (((1,), (1,)), ((), ())), preferred_element_type=f32
    ).astype(bf16)


def combine_kernel(routes_ref, gates_ref, back_ref, out_ref):
    _, slot_cols = route_slots(routes_ref)
    n = out_ref.shape[0]
    slots = back_ref.shape[0] // N_TP
    part = back_ref.shape[1] // N_DP
    eye = iota((n, n), 0) == iota((n, n), 1)
    lane = iota((n, slots), 1)
    picks, gates = [], []
    for k in range(2):
        picks.append(
            jnp.where(lane == slot_cols[k].astype(jnp.int32), 1.0, 0.0).astype(bf16)
        )
        gates.append(
            jnp.sum(jnp.where(eye, gates_ref[k : k + 1, :], 0.0), axis=1, keepdims=True)
        )
    pieces = [None] * (N_TP * N_DP)
    for t in range(N_TP):
        block = back_ref[t * slots : (t + 1) * slots, :]
        mixed = gates[0] * jnp.dot(picks[0], block, preferred_element_type=f32) + gates[
            1
        ] * jnp.dot(picks[1], block, preferred_element_type=f32)
        for i in range(N_DP):
            pieces[i * N_TP + t] = mixed[:, i * part : (i + 1) * part]
    out_ref[...] = jnp.concatenate(pieces, axis=1).astype(bf16)


def split3(x):
    hi = x.astype(bf16)
    rest = x - hi.astype(f32)
    mid = rest.astype(bf16)
    low = (rest - mid.astype(f32)).astype(bf16)
    return hi, mid, low


def attend_kernel(
    where_ref,
    tables_ref,
    lengths_ref,
    a0,
    a1,
    far,
    pool,
    m0,
    m1,
    m2,
    m3,
    o0,
    o1,
    o2,
    o3,
    pages,
    sem,
    asked,
    cache,
    sems,
):
    rank_dp, rank_tp = where_ref[0], where_ref[1]
    source, target, moved = where_ref[2], where_ref[3], where_ref[4]
    copies = [pltpu.make_async_copy(pool, cache, sems.at[N_TP])]
    rows = a0.shape[0]
    pairs = (a0, a1, far.at[pl.ds(0, rows), :], far.at[pl.ds(rows, rows), :])
    for k, a in enumerate(pairs):
        copies.append(pltpu.make_async_copy(a, asked.at[k], sems.at[k]))
    for copy in copies:
        copy.start()
    for rel, m in enumerate((m0, m1, m2, m3)):

        @pl.when(source == (rank_dp ^ rel))
        def _(m=m):
            copy = pltpu.make_async_copy(m, pages, sem)
            copy.start()
            copy.wait()

    for copy in copies:
        copy.wait()
    q0, q1, q2, q3 = [asked[k] for k in range(N_TP)]
    heads = q0.shape[0] // 3
    for s in range(3):
        query = jnp.concatenate(
            [q[s * heads : (s + 1) * heads, :] for q in (q0, q1, q2, q3)], axis=0
        )
        total_heads = query.shape[0]
        length = lengths_ref[s]
        use_moved = (rank_dp == target) & (moved == s)
        keys, scores, valid = [], [], []
        for j in range(SLOTS):
            own = cache[tables_ref[s * SLOTS + j]]
            keys.append(jnp.where(use_moved, pages[j * ROW : (j + 1) * ROW, :], own))
            score = jnp.dot(query, keys[j], preferred_element_type=f32) * score_scale
            place = (j * N_TP + rank_tp) * PAGE + iota(score.shape, 1)
            valid.append(place < length)
            scores.append(jnp.where(valid[j], score, neg_fill))
        top = jnp.max(jnp.maximum(scores[0], scores[1]), axis=1, keepdims=True)
        total = jnp.zeros((total_heads, 1), f32)
        acc = jnp.zeros((total_heads, KV_RANK), f32)
        for j in range(SLOTS):
            weight = jnp.where(valid[j], jnp.exp(scores[j] - top), 0.0).astype(bf16)
            total += jnp.sum(weight.astype(f32), axis=1, keepdims=True)
            acc += lax.dot_general(
                weight, keys[j][:KV_RANK, :], (((1,), (1,)), ((), ())), preferred_element_type=f32
            )
        some = total > 0.0
        safe = jnp.where(some, total, 1.0)
        mean = (acc / safe).astype(bf16)
        level = jnp.where(some, top + jnp.log(safe), neg_fill)
        hi, mid, low = split3(level)
        lane = iota((total_heads, WIDE - KV_RANK), 1)
        tail = jnp.where(
            lane == 0,
            hi.astype(f32),
            jnp.where(lane == 1, mid.astype(f32), jnp.where(lane == 2, low.astype(f32), 0.0)),
        ).astype(bf16)
        for k, o in enumerate((o0, o1, o2, o3)):
            o[s * heads : (s + 1) * heads, :KV_RANK] = mean[k * heads : (k + 1) * heads]
            o[s * heads : (s + 1) * heads, KV_RANK:] = tail[k * heads : (k + 1) * heads]


def merge_kernel(p0, p1, p2, p3, out_ref):
    levels = []
    for p in (p0, p1, p2, p3):
        tail = p[:, KV_RANK:].astype(f32)
        levels.append(tail[:, 0:1] + tail[:, 1:2] + tail[:, 2:3])
    most = jnp.maximum(jnp.maximum(levels[0], levels[1]), jnp.maximum(levels[2], levels[3]))
    numerator = jnp.zeros(out_ref.shape, f32)
    denominator = jnp.zeros((out_ref.shape[0], 1), f32)
    for p, level in zip((p0, p1, p2, p3), levels):
        factor = jnp.exp(level - most)
        denominator += factor
        numerator += factor * p[:, :KV_RANK].astype(f32)
    out_ref[...] = (numerator / denominator).astype(bf16)


def shift(x, k):
    return lax.ppermute(x, "tp", [(i, (i + k) % N_TP) for i in range(N_TP)])


def swap(x, bit):
    return lax.ppermute(x, "dp", [(i, i ^ bit) for i in range(N_DP)])


def per_device(
    queries,
    cache,
    tables,
    lengths,
    mig_cache,
    mig_src,
    mig_dst,
    mig_seq,
    tokens,
    routes,
    gates,
    gate_w,
    up_w,
    down_w,
):
    rank_tp = lax.axis_index("tp")
    rank_dp = lax.axis_index("dp")
    where = jnp.stack([rank_dp, rank_tp, mig_src[0], mig_dst[0], mig_seq[0]]).astype(jnp.int32)
    ranks_ep = lax.axis_size("ep")
    token_rows, width = tokens.shape
    slots_all = ranks_ep * CAP
    quarter = width // 4
    part = gate_w.shape[2]
    routes_t = routes.T
    gates_t = gates.T
    after = lax.optimization_barrier

    sent = pl.pallas_call(
        dispatch_kernel,
        out_shape=jax.ShapeDtypeStruct((slots_all * 4, quarter), bf16),
        in_specs=[ANY] * 2,
        out_specs=VMEM,
        scratch_shapes=[
            pltpu.VMEM(routes_t.shape, routes_t.dtype),
            pltpu.VMEM(tokens.shape, tokens.dtype),
            pltpu.SemaphoreType.DMA((2,)),
        ],
        compiler_params=params(58),
    )(routes_t, tokens)
    arrived = lax.all_to_all(
        sent.reshape(ranks_ep, CAP * 4, quarter), "ep", split_axis=0, concat_axis=0, tiled=True
    ).reshape(slots_all * 4, quarter)

    gate, up, queries, down, pages, _ = after(
        (gate_w[0], up_w[0], queries, down_w[0].T, jnp.swapaxes(mig_cache, 1, 2), sent)
    )
    first = jnp.concatenate([gate, up], axis=0)
    first_x = swap(first, 2)
    first_c = swap(first, 1)
    down_c = swap(down, 1)
    pages = pages.reshape(-1, PAGE)
    heads = queries.shape[1]
    asked = queries.reshape(3 * heads, ROW)
    near = shift(asked, 1)
    far = shift(jnp.concatenate([asked, near], axis=0), 2)
    pages_c = swap(pages, 1)
    arrived, down_c, pages_c, where, near = after((arrived, down_c, pages_c, where, near))

    blocks = [shift(arrived, k) for k in (1, 2, 3)]
    first_x, first_c, far, *blocks = after((first_x, first_c, far, *blocks))
    asks = [near, far]
    first_xc = swap(first_x, 1)
    down_x = swap(after((down, first_x))[0], 2)
    rows = N_TP * slots_all
    hidden = pl.pallas_call(
        hidden_kernel,
        out_shape=jax.ShapeDtypeStruct((N_TP, rows, N_DP * part), bf16),
        in_specs=[SMEM] + [VMEM] * 8,
        out_specs=VMEM,
        scratch_shapes=[pltpu.VMEM((rows, width), bf16)],
        compiler_params=params(24),
    )(where, arrived, *blocks, first, first_c, first_x, first_xc)
    pages_x = swap(after((pages, hidden))[0], 2)
    hiddens = [lax.all_to_all(hidden, "tp", split_axis=0, concat_axis=0, tiled=True)]
    pages_x, *hiddens = after((pages_x, *hiddens))
    down_xc = swap(after((down_x, *hiddens))[0], 1)
    cols = down.shape[0]
    expert_out = pl.pallas_call(
        down_kernel,
        out_shape=jax.ShapeDtypeStruct((rows, N_DP * cols), bf16),
        in_specs=[SMEM] + [VMEM] + [ANY] * 4,
        out_specs=VMEM,
        scratch_shapes=[
            pltpu.VMEM((rows, down.shape[1]), bf16),
            pltpu.VMEM((N_DP * cols, down.shape[1]), bf16),
            pltpu.SemaphoreType.DMA((N_DP,)),
        ],
        compiler_params=params(32),
    )(where, *hiddens, down, down_c, down_x, down_xc)
    returned = lax.all_to_all(
        expert_out.reshape(N_TP * ranks_ep, CAP, N_DP * cols),
        ("tp", "ep"),
        split_axis=0,
        concat_axis=0,
        tiled=True,
    ).reshape(rows, N_DP * cols)

    pages_xc = swap(pages_x, 1)
    parts = pl.pallas_call(
        attend_kernel,
        out_shape=[jax.ShapeDtypeStruct((3 * heads, WIDE), bf16)] * 4,
        in_specs=[SMEM] * 3 + [ANY] * 8,
        out_specs=[VMEM] * 4,
        scratch_shapes=[
            pltpu.VMEM((SLOTS * ROW, PAGE), bf16),
            pltpu.SemaphoreType.DMA,
            pltpu.VMEM((N_TP,) + asked.shape, bf16),
            pltpu.VMEM((cache.shape[0], ROW, PAGE), bf16),
            pltpu.SemaphoreType.DMA((N_TP + 1,)),
        ],
        compiler_params=params(32),
    )(
        where,
        tables.reshape(-1),
        lengths.reshape(-1),
        asked,
        *asks,
        jnp.swapaxes(cache, 1, 2),
        pages,
        pages_c,
        pages_x,
        pages_xc,
    )
    merged = pl.pallas_call(
        merge_kernel,
        out_shape=jax.ShapeDtypeStruct((3 * heads, KV_RANK), bf16),
        in_specs=[VMEM] * 4,
        out_specs=VMEM,
        compiler_params=params(16),
    )(parts[0], *[shift(parts[k], -k) for k in (1, 2, 3)])
    attn_out = merged.reshape(3, heads, KV_RANK)
    moe_out = pl.pallas_call(
        combine_kernel,
        out_shape=jax.ShapeDtypeStruct((token_rows, width), bf16),
        in_specs=[VMEM] * 3,
        out_specs=VMEM,
        compiler_params=params(16),
    )(routes_t, gates_t, returned)
    return (attn_out, moe_out)


def solution(mesh):
    in_specs = (
        P(("dp", "ep"), "tp", None),
        P(("dp", "tp", "ep"), None, None),
        P(("dp", "tp", "ep"), None),
        P("dp", "ep", None),
        P(("dp", "tp", "ep"), None, None),
        P("ep"),
        P("ep"),
        P("ep"),
        P(("dp", "tp", "ep"), None),
        P(("dp", "tp", "ep"), None),
        P(("dp", "tp", "ep"), None),
        P("ep", None, ("dp", "tp")),
        P("ep", None, ("dp", "tp")),
        P("ep", None, ("dp", "tp")),
    )
    out_specs = (P(("dp", "ep"), "tp", None), P(("dp", "tp", "ep"), None))
    return jax.shard_map(
        per_device, mesh=mesh, in_specs=in_specs, out_specs=out_specs, check_vma=False
    )
```

```python
import jax
import jax.numpy as jnp
from jax import lax
from jax.experimental import pallas as pl
from jax.experimental.pallas import tpu as pltpu
from jax.sharding import PartitionSpec as P

KV_RANK = 512
ROPE_DIM = 64
PAGE = 128
SLOTS = 2
ROW = KV_RANK + ROPE_DIM
WIDE = 640
CAP = 2
N_TP = 4
N_DP = 4
BLOCK_SHIFTS = (0, 2, 1, 3)

score_scale = 0.07216878364870322
neg_fill = -1e30
f32 = jnp.float32
bf16 = jnp.bfloat16

VMEM = pl.BlockSpec(memory_space=pltpu.VMEM)
SMEM = pl.BlockSpec(memory_space=pltpu.SMEM)
ANY = pl.BlockSpec(memory_space=pl.ANY)


def params(mib):
    return pltpu.CompilerParams(vmem_limit_bytes=mib << 20)


def iota(shape, dim):
    return lax.broadcasted_iota(jnp.int32, shape, dim)


def route_slots(routes_ref):
    n = routes_ref.shape[1]
    sub, lane = iota((n, n), 0), iota((n, n), 1)
    rows = [routes_ref[k : k + 1, :].astype(f32) for k in range(2)]
    cols = [jnp.sum(jnp.where(sub == lane, r, 0.0), axis=1, keepdims=True) for r in rows]
    slot_rows, slot_cols = [], []
    for k in range(2):
        hits = jnp.where(cols[0] == rows[k], 1.0, 0.0) + jnp.where(cols[1] == rows[k], 1.0, 0.0)
        count = jnp.sum(jnp.where(sub < lane, hits, 0.0), axis=0, keepdims=True)
        slot_rows.append(rows[k] * CAP + count)
        hits = jnp.where(rows[0] == cols[k], 1.0, 0.0) + jnp.where(rows[1] == cols[k], 1.0, 0.0)
        count = jnp.sum(jnp.where(lane < sub, hits, 0.0), axis=1, keepdims=True)
        slot_cols.append(cols[k] * CAP + count)
    return slot_rows, slot_cols


def dispatch_kernel(routes_any, tok_any, out_ref, routes_ref, tok_ref, sems):
    copies = [
        pltpu.make_async_copy(routes_any, routes_ref, sems.at[0]),
        pltpu.make_async_copy(tok_any, tok_ref, sems.at[1]),
    ]
    for copy in copies:
        copy.start()
    for copy in copies:
        copy.wait()
    slot_rows, _ = route_slots(routes_ref)
    rows, quarter = out_ref.shape
    n = tok_ref.shape[0]
    place = iota((rows, n), 0)
    total = jnp.zeros((rows, quarter), f32)
    for q in range(4):
        t0 = slot_rows[0].astype(jnp.int32) * 4 + q
        t1 = slot_rows[1].astype(jnp.int32) * 4 + q
        pick = jnp.where((place == t0) | (place == t1), 1.0, 0.0).astype(bf16)
        total += jnp.dot(
            pick, tok_ref[:, q * quarter : (q + 1) * quarter], preferred_element_type=f32
        )
    out_ref[...] = total.astype(bf16)


def hidden_kernel(where_ref, b0, b1, b2, b3, w0, w1, w2, w3, out_ref, rows_ref):
    rank_dp, rank_tp = where_ref[0], where_ref[1]
    depth, part = w0.shape[0] // 2, w0.shape[1]
    count, quarter = b0.shape
    slots = count // 4
    for k, b in zip(BLOCK_SHIFTS, (b0, b1, b2, b3)):
        base = pl.multiple_of(((rank_tp + N_TP - k) % N_TP) * slots, slots)
        block = b[...]
        row = iota((count, count), 0)
        pick = jnp.where(
            iota((count, count), 1) == (row % slots) * 4 + row // slots, 1.0, 0.0
        ).astype(bf16)
        sorted_rows = jnp.dot(pick, block, preferred_element_type=f32).astype(bf16)
        for q in range(4):
            rows_ref[pl.ds(base, slots), q * quarter : (q + 1) * quarter] = sorted_rows[
                q * slots : (q + 1) * slots
            ]
    for rel, w in enumerate((w0, w1, w2, w3)):
        both = jnp.dot(
            rows_ref[...],
            jnp.concatenate([w[:depth, :], w[depth:, :]], axis=1),
            preferred_element_type=f32,
        )
        gate, up = both[:, :part], both[:, part:]
        hidden = (gate / (1.0 + jnp.exp(-gate)) * up).astype(bf16)
        base = pl.multiple_of((rank_dp ^ rel) * part, part)
        for copy in range(out_ref.shape[0]):
            out_ref[copy, :, pl.ds(base, part)] = hidden


def down_kernel(where_ref, parts, d0, d1, d2, d3, out_ref, hidden, weights, sems):
    rank_dp = where_ref[0]
    cols = d0.shape[0]
    part = parts.shape[2] // N_DP
    copies = []
    for rel, d in enumerate((d0, d1, d2, d3)):
        base = pl.multiple_of((rank_dp ^ rel) * cols, 16)
        copy = pltpu.make_async_copy(d, weights.at[pl.ds(base, cols), :], sems.at[rel])
        copy.start()
        copies.append(copy)
    for t in range(N_TP):
        for i in range(N_DP):
            base = (i * N_TP + t) * part
            hidden[:, base : base + part] = parts[t, :, i * part : (i + 1) * part]
    for copy in copies:
        copy.wait()
    out_ref[...] = lax.dot_general(
        hidden[...], weights[...], (((1,), (1,)), ((), ())), preferred_element_type=f32
    ).astype(bf16)


def combine_kernel(routes_ref, gates_ref, back_ref, out_ref):
    _, slot_cols = route_slots(routes_ref)
    n = out_ref.shape[0]
    slots = back_ref.shape[0] // N_TP
    part = back_ref.shape[1] // N_DP
    eye = iota((n, n), 0) == iota((n, n), 1)
    lane = iota((n, slots), 1)
    picks, gates = [], []
    for k in range(2):
        picks.append(
            jnp.where(lane == slot_cols[k].astype(jnp.int32), 1.0, 0.0).astype(bf16)
        )
        gates.append(
            jnp.sum(jnp.where(eye, gates_ref[k : k + 1, :], 0.0), axis=1, keepdims=True)
        )
    pieces = [None] * (N_TP * N_DP)
    for t in range(N_TP):
        block = back_ref[t * slots : (t + 1) * slots, :]
        mixed = gates[0] * jnp.dot(picks[0], block, preferred_element_type=f32) + gates[
            1
        ] * jnp.dot(picks[1], block, preferred_element_type=f32)
        for i in range(N_DP):
            pieces[i * N_TP + t] = mixed[:, i * part : (i + 1) * part]
    out_ref[...] = jnp.concatenate(pieces, axis=1).astype(bf16)


def split3(x):
    hi = x.astype(bf16)
    rest = x - hi.astype(f32)
    mid = rest.astype(bf16)
    low = (rest - mid.astype(f32)).astype(bf16)
    return hi, mid, low


def attend_kernel(
    where_ref,
    tables_ref,
    lengths_ref,
    a0,
    a1,
    far,
    pool,
    m0,
    m1,
    m2,
    m3,
    o0,
    o1,
    o2,
    o3,
    pages,
    sem,
    asked,
    cache,
    sems,
):
    rank_dp, rank_tp = where_ref[0], where_ref[1]
    source, target, moved = where_ref[2], where_ref[3], where_ref[4]
    copies = [pltpu.make_async_copy(pool, cache, sems.at[N_TP])]
    rows = a0.shape[0]
    pairs = (a0, a1, far.at[pl.ds(0, rows), :], far.at[pl.ds(rows, rows), :])
    for k, a in enumerate(pairs):
        copies.append(pltpu.make_async_copy(a, asked.at[k], sems.at[k]))
    for copy in copies:
        copy.start()
    for rel, m in enumerate((m0, m1, m2, m3)):

        @pl.when(source == (rank_dp ^ rel))
        def _(m=m):
            copy = pltpu.make_async_copy(m, pages, sem)
            copy.start()
            copy.wait()

    for copy in copies:
        copy.wait()
    q0, q1, q2, q3 = [asked[k] for k in range(N_TP)]
    heads = q0.shape[0] // 3
    for s in range(3):
        query = jnp.concatenate(
            [q[s * heads : (s + 1) * heads, :] for q in (q0, q1, q2, q3)], axis=0
        )
        total_heads = query.shape[0]
        length = lengths_ref[s]
        use_moved = (rank_dp == target) & (moved == s)
        keys, scores, valid = [], [], []
        for j in range(SLOTS):
            own = cache[tables_ref[s * SLOTS + j]]
            keys.append(jnp.where(use_moved, pages[j * ROW : (j + 1) * ROW, :], own))
            score = jnp.dot(query, keys[j], preferred_element_type=f32) * score_scale
            place = (j * N_TP + rank_tp) * PAGE + iota(score.shape, 1)
            valid.append(place < length)
            scores.append(jnp.where(valid[j], score, neg_fill))
        top = jnp.max(jnp.maximum(scores[0], scores[1]), axis=1, keepdims=True)
        total = jnp.zeros((total_heads, 1), f32)
        acc = jnp.zeros((total_heads, KV_RANK), f32)
        for j in range(SLOTS):
            weight = jnp.where(valid[j], jnp.exp(scores[j] - top), 0.0).astype(bf16)
            total += jnp.sum(weight.astype(f32), axis=1, keepdims=True)
            acc += lax.dot_general(
                weight, keys[j][:KV_RANK, :], (((1,), (1,)), ((), ())), preferred_element_type=f32
            )
        some = total > 0.0
        safe = jnp.where(some, total, 1.0)
        mean = (acc / safe).astype(bf16)
        level = jnp.where(some, top + jnp.log(safe), neg_fill)
        hi, mid, low = split3(level)
        lane = iota((total_heads, WIDE - KV_RANK), 1)
        tail = jnp.where(
            lane == 0,
            hi.astype(f32),
            jnp.where(lane == 1, mid.astype(f32), jnp.where(lane == 2, low.astype(f32), 0.0)),
        ).astype(bf16)
        for k, o in enumerate((o0, o1, o2, o3)):
            o[s * heads : (s + 1) * heads, :KV_RANK] = mean[k * heads : (k + 1) * heads]
            o[s * heads : (s + 1) * heads, KV_RANK:] = tail[k * heads : (k + 1) * heads]


def merge_kernel(p0, p1, p2, p3, out_ref):
    levels = []
    for p in (p0, p1, p2, p3):
        tail = p[:, KV_RANK:].astype(f32)
        levels.append(tail[:, 0:1] + tail[:, 1:2] + tail[:, 2:3])
    most = jnp.maximum(jnp.maximum(levels[0], levels[1]), jnp.maximum(levels[2], levels[3]))
    numerator = jnp.zeros(out_ref.shape, f32)
    denominator = jnp.zeros((out_ref.shape[0], 1), f32)
    for p, level in zip((p0, p1, p2, p3), levels):
        factor = jnp.exp(level - most)
        denominator += factor
        numerator += factor * p[:, :KV_RANK].astype(f32)
    out_ref[...] = (numerator / denominator).astype(bf16)


def shift(x, k):
    return lax.ppermute(x, "tp", [(i, (i + k) % N_TP) for i in range(N_TP)])


def swap(x, bit):
    return lax.ppermute(x, "dp", [(i, i ^ bit) for i in range(N_DP)])


def per_device(
    queries,
    cache,
    tables,
    lengths,
    mig_cache,
    mig_src,
    mig_dst,
    mig_seq,
    tokens,
    routes,
    gates,
    gate_w,
    up_w,
    down_w,
):
    rank_tp = lax.axis_index("tp")
    rank_dp = lax.axis_index("dp")
    where = jnp.stack([rank_dp, rank_tp, mig_src[0], mig_dst[0], mig_seq[0]]).astype(jnp.int32)
    ranks_ep = lax.axis_size("ep")
    token_rows, width = tokens.shape
    slots_all = ranks_ep * CAP
    quarter = width // 4
    part = gate_w.shape[2]
    routes_t = routes.T
    gates_t = gates.T
    after = lax.optimization_barrier

    sent = pl.pallas_call(
        dispatch_kernel,
        out_shape=jax.ShapeDtypeStruct((slots_all * 4, quarter), bf16),
        in_specs=[ANY] * 2,
        out_specs=VMEM,
        scratch_shapes=[
            pltpu.VMEM(routes_t.shape, routes_t.dtype),
            pltpu.VMEM(tokens.shape, tokens.dtype),
            pltpu.SemaphoreType.DMA((2,)),
        ],
        compiler_params=params(58),
    )(routes_t, tokens)
    arrived = lax.all_to_all(
        sent.reshape(ranks_ep, CAP * 4, quarter), "ep", split_axis=0, concat_axis=0, tiled=True
    ).reshape(slots_all * 4, quarter)

    gate, up, queries, down, pages, _ = after(
        (gate_w[0], up_w[0], queries, down_w[0].T, jnp.swapaxes(mig_cache, 1, 2), sent)
    )
    first = jnp.concatenate([gate, up], axis=0)
    first_x = swap(first, 2)
    first_c = swap(first, 1)
    down_c = swap(down, 1)
    pages = pages.reshape(-1, PAGE)
    heads = queries.shape[1]
    asked = queries.reshape(3 * heads, ROW)
    near = shift(asked, 1)
    far = shift(jnp.concatenate([asked, near], axis=0), 2)
    pages_c = swap(pages, 1)
    arrived, down_c, pages_c, where, near = after((arrived, down_c, pages_c, where, near))

    blocks = [shift(arrived, k) for k in BLOCK_SHIFTS[1:]]
    first_x, first_c, far, *blocks = after((first_x, first_c, far, *blocks))
    asks = [near, far]
    first_xc = swap(first_x, 1)
    down_x = swap(after((down, first_x))[0], 2)
    rows = N_TP * slots_all
    hidden = pl.pallas_call(
        hidden_kernel,
        out_shape=jax.ShapeDtypeStruct((N_TP, rows, N_DP * part), bf16),
        in_specs=[SMEM] + [VMEM] * 8,
        out_specs=VMEM,
        scratch_shapes=[pltpu.VMEM((rows, width), bf16)],
        compiler_params=params(24),
    )(where, arrived, *blocks, first, first_c, first_x, first_xc)
    pages_x = swap(after((pages, hidden))[0], 2)
    hiddens = [lax.all_to_all(hidden, "tp", split_axis=0, concat_axis=0, tiled=True)]
    pages_x, *hiddens = after((pages_x, *hiddens))
    down_xc = swap(after((down_x, *hiddens))[0], 1)
    cols = down.shape[0]
    expert_out = pl.pallas_call(
        down_kernel,
        out_shape=jax.ShapeDtypeStruct((rows, N_DP * cols), bf16),
        in_specs=[SMEM] + [VMEM] + [ANY] * 4,
        out_specs=VMEM,
        scratch_shapes=[
            pltpu.VMEM((rows, down.shape[1]), bf16),
            pltpu.VMEM((N_DP * cols, down.shape[1]), bf16),
            pltpu.SemaphoreType.DMA((N_DP,)),
        ],
        compiler_params=params(32),
    )(where, *hiddens, down, down_c, down_x, down_xc)
    returned = lax.all_to_all(
        expert_out.reshape(N_TP * ranks_ep, CAP, N_DP * cols),
        ("tp", "ep"),
        split_axis=0,
        concat_axis=0,
        tiled=True,
    ).reshape(rows, N_DP * cols)

    pages_xc = swap(pages_x, 1)
    parts = pl.pallas_call(
        attend_kernel,
        out_shape=[jax.ShapeDtypeStruct((3 * heads, WIDE), bf16)] * 4,
        in_specs=[SMEM] * 3 + [ANY] * 8,
        out_specs=[VMEM] * 4,
        scratch_shapes=[
            pltpu.VMEM((SLOTS * ROW, PAGE), bf16),
            pltpu.SemaphoreType.DMA,
            pltpu.VMEM((N_TP,) + asked.shape, bf16),
            pltpu.VMEM((cache.shape[0], ROW, PAGE), bf16),
            pltpu.SemaphoreType.DMA((N_TP + 1,)),
        ],
        compiler_params=params(32),
    )(
        where,
        tables.reshape(-1),
        lengths.reshape(-1),
        asked,
        *asks,
        jnp.swapaxes(cache, 1, 2),
        pages,
        pages_c,
        pages_x,
        pages_xc,
    )
    merged = pl.pallas_call(
        merge_kernel,
        out_shape=jax.ShapeDtypeStruct((3 * heads, KV_RANK), bf16),
        in_specs=[VMEM] * 4,
        out_specs=VMEM,
        compiler_params=params(16),
    )(parts[0], *[shift(parts[k], -k) for k in (1, 2, 3)])
    attn_out = merged.reshape(3, heads, KV_RANK)
    moe_out = pl.pallas_call(
        combine_kernel,
        out_shape=jax.ShapeDtypeStruct((token_rows, width), bf16),
        in_specs=[VMEM] * 3,
        out_specs=VMEM,
        compiler_params=params(16),
    )(routes_t, gates_t, returned)
    return (attn_out, moe_out)


def solution(mesh):
    in_specs = (
        P(("dp", "ep"), "tp", None),
        P(("dp", "tp", "ep"), None, None),
        P(("dp", "tp", "ep"), None),
        P("dp", "ep", None),
        P(("dp", "tp", "ep"), None, None),
        P("ep"),
        P("ep"),
        P("ep"),
        P(("dp", "tp", "ep"), None),
        P(("dp", "tp", "ep"), None),
        P(("dp", "tp", "ep"), None),
        P("ep", None, ("dp", "tp")),
        P("ep", None, ("dp", "tp")),
        P("ep", None, ("dp", "tp")),
    )
    out_specs = (P(("dp", "ep"), "tp", None), P(("dp", "tp", "ep"), None))
    return jax.shard_map(
        per_device, mesh=mesh, in_specs=in_specs, out_specs=out_specs, check_vma=False
    )
```

```python
import jax
import jax.numpy as jnp
from jax import lax
from jax.experimental import pallas as pl
from jax.experimental.pallas import tpu as pltpu
from jax.sharding import PartitionSpec as P

KV_RANK = 512
ROPE_DIM = 64
PAGE = 128
SLOTS = 2
ROW = KV_RANK + ROPE_DIM
WIDE = 640
CAP = 2
N_TP = 4
N_DP = 4
BLOCK_SHIFTS = (0, 2, 1, 3)

score_scale = 0.07216878364870322
neg_fill = -1e30
f32 = jnp.float32
bf16 = jnp.bfloat16

VMEM = pl.BlockSpec(memory_space=pltpu.VMEM)
SMEM = pl.BlockSpec(memory_space=pltpu.SMEM)
ANY = pl.BlockSpec(memory_space=pl.ANY)


def params(mib):
    return pltpu.CompilerParams(vmem_limit_bytes=mib << 20)


def iota(shape, dim):
    return lax.broadcasted_iota(jnp.int32, shape, dim)


def route_slots(routes_ref):
    n = routes_ref.shape[1]
    sub, lane = iota((n, n), 0), iota((n, n), 1)
    rows = [routes_ref[k : k + 1, :].astype(f32) for k in range(2)]
    cols = [jnp.sum(jnp.where(sub == lane, r, 0.0), axis=1, keepdims=True) for r in rows]
    slot_rows, slot_cols = [], []
    for k in range(2):
        hits = jnp.where(cols[0] == rows[k], 1.0, 0.0) + jnp.where(cols[1] == rows[k], 1.0, 0.0)
        count = jnp.sum(jnp.where(sub < lane, hits, 0.0), axis=0, keepdims=True)
        slot_rows.append(rows[k] * CAP + count)
        hits = jnp.where(rows[0] == cols[k], 1.0, 0.0) + jnp.where(rows[1] == cols[k], 1.0, 0.0)
        count = jnp.sum(jnp.where(lane < sub, hits, 0.0), axis=1, keepdims=True)
        slot_cols.append(cols[k] * CAP + count)
    return slot_rows, slot_cols


def dispatch_kernel(routes_any, tok_any, out_ref, routes_ref, tok_ref, sems):
    copies = [
        pltpu.make_async_copy(routes_any, routes_ref, sems.at[0]),
        pltpu.make_async_copy(tok_any, tok_ref, sems.at[1]),
    ]
    for copy in copies:
        copy.start()
    for copy in copies:
        copy.wait()
    slot_rows, _ = route_slots(routes_ref)
    rows, quarter = out_ref.shape
    n = tok_ref.shape[0]
    place = iota((rows, n), 0)
    total = jnp.zeros((rows, quarter), f32)
    for q in range(4):
        t0 = slot_rows[0].astype(jnp.int32) * 4 + q
        t1 = slot_rows[1].astype(jnp.int32) * 4 + q
        pick = jnp.where((place == t0) | (place == t1), 1.0, 0.0).astype(bf16)
        total += jnp.dot(
            pick, tok_ref[:, q * quarter : (q + 1) * quarter], preferred_element_type=f32
        )
    out_ref[...] = total.astype(bf16)


def hidden_kernel(where_ref, b0, b1, b2, b3, w0, w1, w2, w3, out_ref, rows_ref):
    rank_dp, rank_tp = where_ref[0], where_ref[1]
    depth, part = w0.shape[0] // 2, w0.shape[1]
    count, quarter = b0.shape
    slots = count // 4
    for k, b in zip(BLOCK_SHIFTS, (b0, b1, b2, b3)):
        base = pl.multiple_of(((rank_tp + N_TP - k) % N_TP) * slots, slots)
        block = b[...]
        row = iota((count, count), 0)
        pick = jnp.where(
            iota((count, count), 1) == (row % slots) * 4 + row // slots, 1.0, 0.0
        ).astype(bf16)
        sorted_rows = jnp.dot(pick, block, preferred_element_type=f32).astype(bf16)
        for q in range(4):
            rows_ref[pl.ds(base, slots), q * quarter : (q + 1) * quarter] = sorted_rows[
                q * slots : (q + 1) * slots
            ]
    for rel, w in enumerate((w0, w1, w2, w3)):
        both = jnp.dot(
            rows_ref[...],
            jnp.concatenate([w[:depth, :], w[depth:, :]], axis=1),
            preferred_element_type=f32,
        )
        gate, up = both[:, :part], both[:, part:]
        hidden = (gate / (1.0 + jnp.exp(-gate)) * up).astype(bf16)
        base = pl.multiple_of((rank_dp ^ rel) * part, part)
        for copy in range(out_ref.shape[0]):
            out_ref[copy, :, pl.ds(base, part)] = hidden


def down_kernel(where_ref, parts, d0, d1, d2, d3, out_ref, hidden, weights, sems):
    rank_dp = where_ref[0]
    cols = d0.shape[0]
    part = parts.shape[2] // N_DP
    copies = []
    for rel, d in enumerate((d0, d1, d2, d3)):
        base = pl.multiple_of((rank_dp ^ rel) * cols, 16)
        copy = pltpu.make_async_copy(d, weights.at[pl.ds(base, cols), :], sems.at[rel])
        copy.start()
        copies.append(copy)
    for t in range(N_TP):
        for i in range(N_DP):
            base = (i * N_TP + t) * part
            hidden[:, base : base + part] = parts[t, :, i * part : (i + 1) * part]
    for copy in copies:
        copy.wait()
    out_ref[...] = lax.dot_general(
        hidden[...], weights[...], (((1,), (1,)), ((), ())), preferred_element_type=f32
    ).astype(bf16)


def combine_kernel(routes_ref, gates_ref, back_ref, out_ref):
    _, slot_cols = route_slots(routes_ref)
    n = out_ref.shape[0]
    slots = back_ref.shape[0] // N_TP
    part = back_ref.shape[1] // N_DP
    eye = iota((n, n), 0) == iota((n, n), 1)
    lane = iota((n, slots), 1)
    picks, gates = [], []
    for k in range(2):
        picks.append(
            jnp.where(lane == slot_cols[k].astype(jnp.int32), 1.0, 0.0).astype(bf16)
        )
        gates.append(
            jnp.sum(jnp.where(eye, gates_ref[k : k + 1, :], 0.0), axis=1, keepdims=True)
        )
    pieces = [None] * (N_TP * N_DP)
    for t in range(N_TP):
        block = back_ref[t * slots : (t + 1) * slots, :]
        mixed = gates[0] * jnp.dot(picks[0], block, preferred_element_type=f32) + gates[
            1
        ] * jnp.dot(picks[1], block, preferred_element_type=f32)
        for i in range(N_DP):
            pieces[i * N_TP + t] = mixed[:, i * part : (i + 1) * part]
    out_ref[...] = jnp.concatenate(pieces, axis=1).astype(bf16)


def split3(x):
    hi = x.astype(bf16)
    rest = x - hi.astype(f32)
    mid = rest.astype(bf16)
    low = (rest - mid.astype(f32)).astype(bf16)
    return hi, mid, low


def attend_kernel(
    where_ref,
    tables_ref,
    lengths_ref,
    a0,
    a1,
    far,
    pool,
    m0,
    m1,
    m2,
    m3,
    o0,
    o1,
    o2,
    o3,
    pages,
    sem,
    asked,
    cache,
    sems,
):
    rank_dp, rank_tp = where_ref[0], where_ref[1]
    source, target, moved = where_ref[2], where_ref[3], where_ref[4]
    copies = [pltpu.make_async_copy(pool, cache, sems.at[N_TP])]
    rows = a0.shape[0]
    pairs = (a0, a1, far.at[pl.ds(0, rows), :], far.at[pl.ds(rows, rows), :])
    for k, a in enumerate(pairs):
        copies.append(pltpu.make_async_copy(a, asked.at[k], sems.at[k]))
    for copy in copies:
        copy.start()
    for rel, m in enumerate((m0, m1, m2, m3)):

        @pl.when(source == (rank_dp ^ rel))
        def _(m=m):
            copy = pltpu.make_async_copy(m, pages, sem)
            copy.start()
            copy.wait()

    for copy in copies:
        copy.wait()
    q0, q1, q2, q3 = [asked[k] for k in range(N_TP)]
    heads = q0.shape[0] // 3
    for s in range(3):
        query = jnp.concatenate(
            [q[s * heads : (s + 1) * heads, :] for q in (q0, q1, q2, q3)], axis=0
        )
        total_heads = query.shape[0]
        length = lengths_ref[s]
        use_moved = (rank_dp == target) & (moved == s)
        keys, scores, valid = [], [], []
        for j in range(SLOTS):
            own = cache[tables_ref[s * SLOTS + j]]
            keys.append(jnp.where(use_moved, pages[j * ROW : (j + 1) * ROW, :], own))
            score = jnp.dot(query, keys[j], preferred_element_type=f32) * score_scale
            place = (j * N_TP + rank_tp) * PAGE + iota(score.shape, 1)
            valid.append(place < length)
            scores.append(jnp.where(valid[j], score, neg_fill))
        top = jnp.max(jnp.maximum(scores[0], scores[1]), axis=1, keepdims=True)
        total = jnp.zeros((total_heads, 1), f32)
        acc = jnp.zeros((total_heads, KV_RANK), f32)
        for j in range(SLOTS):
            weight = jnp.where(valid[j], jnp.exp(scores[j] - top), 0.0).astype(bf16)
            total += jnp.sum(weight.astype(f32), axis=1, keepdims=True)
            acc += lax.dot_general(
                weight, keys[j][:KV_RANK, :], (((1,), (1,)), ((), ())), preferred_element_type=f32
            )
        some = total > 0.0
        safe = jnp.where(some, total, 1.0)
        mean = (acc / safe).astype(bf16)
        level = jnp.where(some, top + jnp.log(safe), neg_fill)
        hi, mid, low = split3(level)
        lane = iota((total_heads, WIDE - KV_RANK), 1)
        tail = jnp.where(
            lane == 0,
            hi.astype(f32),
            jnp.where(lane == 1, mid.astype(f32), jnp.where(lane == 2, low.astype(f32), 0.0)),
        ).astype(bf16)
        for k, o in enumerate((o0, o1, o2, o3)):
            o[s * heads : (s + 1) * heads, :KV_RANK] = mean[k * heads : (k + 1) * heads]
            o[s * heads : (s + 1) * heads, KV_RANK:] = tail[k * heads : (k + 1) * heads]


def merge_kernel(p0, p1, p2, p3, out_ref):
    levels = []
    for p in (p0, p1, p2, p3):
        tail = p[:, KV_RANK:].astype(f32)
        levels.append(tail[:, 0:1] + tail[:, 1:2] + tail[:, 2:3])
    most = jnp.maximum(jnp.maximum(levels[0], levels[1]), jnp.maximum(levels[2], levels[3]))
    numerator = jnp.zeros(out_ref.shape, f32)
    denominator = jnp.zeros((out_ref.shape[0], 1), f32)
    for p, level in zip((p0, p1, p2, p3), levels):
        factor = jnp.exp(level - most)
        denominator += factor
        numerator += factor * p[:, :KV_RANK].astype(f32)
    out_ref[...] = (numerator / denominator).astype(bf16)


def shift(x, k):
    return lax.ppermute(x, "tp", [(i, (i + k) % N_TP) for i in range(N_TP)])


def swap(x, bit):
    return lax.ppermute(x, "dp", [(i, i ^ bit) for i in range(N_DP)])


def per_device(
    queries,
    cache,
    tables,
    lengths,
    mig_cache,
    mig_src,
    mig_dst,
    mig_seq,
    tokens,
    routes,
    gates,
    gate_w,
    up_w,
    down_w,
):
    rank_tp = lax.axis_index("tp")
    rank_dp = lax.axis_index("dp")
    where = jnp.stack([rank_dp, rank_tp, mig_src[0], mig_dst[0], mig_seq[0]]).astype(jnp.int32)
    ranks_ep = lax.axis_size("ep")
    token_rows, width = tokens.shape
    slots_all = ranks_ep * CAP
    quarter = width // 4
    part = gate_w.shape[2]
    routes_t = routes.T
    gates_t = gates.T
    after = lax.optimization_barrier

    sent = pl.pallas_call(
        dispatch_kernel,
        out_shape=jax.ShapeDtypeStruct((slots_all * 4, quarter), bf16),
        in_specs=[ANY] * 2,
        out_specs=VMEM,
        scratch_shapes=[
            pltpu.VMEM(routes_t.shape, routes_t.dtype),
            pltpu.VMEM(tokens.shape, tokens.dtype),
            pltpu.SemaphoreType.DMA((2,)),
        ],
        compiler_params=params(58),
    )(routes_t, tokens)
    arrived = lax.all_to_all(
        sent.reshape(ranks_ep, CAP * 4, quarter), "ep", split_axis=0, concat_axis=0, tiled=True
    ).reshape(slots_all * 4, quarter)

    gate, up, queries, down, pages, _ = after(
        (gate_w[0], up_w[0], queries, down_w[0].T, jnp.swapaxes(mig_cache, 1, 2), sent)
    )
    first = jnp.concatenate([gate, up], axis=0)
    first_x = swap(first, 2)
    first_c = swap(first, 1)
    down_c = swap(down, 1)
    pages = pages.reshape(-1, PAGE)
    heads = queries.shape[1]
    asked = queries.reshape(3 * heads, ROW)
    near = shift(asked, 1)
    far = shift(jnp.concatenate([asked, near], axis=0), 2)
    pages_c = swap(pages, 1)
    arrived, down_c, pages_c, where, near = after((arrived, down_c, pages_c, where, near))

    blocks = [shift(arrived, k) for k in BLOCK_SHIFTS[1:]]
    first_x, first_c, far, *blocks = after((first_x, first_c, far, *blocks))
    asks = [near, far]
    first_xc = swap(first_x, 1)
    down_x = swap(after((down, first_x))[0], 2)
    rows = N_TP * slots_all
    hidden = pl.pallas_call(
        hidden_kernel,
        out_shape=jax.ShapeDtypeStruct((N_TP, rows, N_DP * part), bf16),
        in_specs=[SMEM] + [VMEM] * 8,
        out_specs=VMEM,
        scratch_shapes=[pltpu.VMEM((rows, width), bf16)],
        compiler_params=params(24),
    )(where, arrived, *blocks, first, first_c, first_x, first_xc)
    pages_x = swap(after((pages, hidden))[0], 2)
    hiddens = [lax.all_to_all(hidden, "tp", split_axis=0, concat_axis=0, tiled=True)]
    pages_x, *hiddens = after((pages_x, *hiddens))
    down_xc = swap(after((down_x, *hiddens))[0], 1)
    cols = down.shape[0]
    expert_out = pl.pallas_call(
        down_kernel,
        out_shape=jax.ShapeDtypeStruct((rows, N_DP * cols), bf16),
        in_specs=[SMEM] + [VMEM] + [ANY] * 4,
        out_specs=VMEM,
        scratch_shapes=[
            pltpu.VMEM((rows, down.shape[1]), bf16),
            pltpu.VMEM((N_DP * cols, down.shape[1]), bf16),
            pltpu.SemaphoreType.DMA((N_DP,)),
        ],
        compiler_params=params(32),
    )(where, *hiddens, down, down_c, down_x, down_xc)
    returned = lax.all_to_all(
        expert_out.reshape(N_TP * ranks_ep, CAP, N_DP * cols),
        ("tp", "ep"),
        split_axis=0,
        concat_axis=0,
        tiled=True,
    ).reshape(rows, N_DP * cols)

    pages_xc = swap(pages_x, 1)
    parts = pl.pallas_call(
        attend_kernel,
        out_shape=[jax.ShapeDtypeStruct((3 * heads, WIDE), bf16)] * 4,
        in_specs=[SMEM] * 3 + [ANY] * 8,
        out_specs=[VMEM] * 4,
        scratch_shapes=[
            pltpu.VMEM((SLOTS * ROW, PAGE), bf16),
            pltpu.SemaphoreType.DMA,
            pltpu.VMEM((N_TP,) + asked.shape, bf16),
            pltpu.VMEM((cache.shape[0], ROW, PAGE), bf16),
            pltpu.SemaphoreType.DMA((N_TP + 1,)),
        ],
        compiler_params=params(32),
    )(
        where,
        tables.reshape(-1),
        lengths.reshape(-1),
        asked,
        *asks,
        jnp.swapaxes(cache, 1, 2),
        pages,
        pages_c,
        pages_x,
        pages_xc,
    )
    merged = pl.pallas_call(
        merge_kernel,
        out_shape=jax.ShapeDtypeStruct((3 * heads, KV_RANK), bf16),
        in_specs=[VMEM] * 4,
        out_specs=VMEM,
        compiler_params=params(16),
    )(parts[0], *[shift(parts[k], -k) for k in BLOCK_SHIFTS[1:]])
    attn_out = merged.reshape(3, heads, KV_RANK)
    moe_out = pl.pallas_call(
        combine_kernel,
        out_shape=jax.ShapeDtypeStruct((token_rows, width), bf16),
        in_specs=[VMEM] * 3,
        out_specs=VMEM,
        compiler_params=params(16),
    )(routes_t, gates_t, returned)
    return (attn_out, moe_out)


def solution(mesh):
    in_specs = (
        P(("dp", "ep"), "tp", None),
        P(("dp", "tp", "ep"), None, None),
        P(("dp", "tp", "ep"), None),
        P("dp", "ep", None),
        P(("dp", "tp", "ep"), None, None),
        P("ep"),
        P("ep"),
        P("ep"),
        P(("dp", "tp", "ep"), None),
        P(("dp", "tp", "ep"), None),
        P(("dp", "tp", "ep"), None),
        P("ep", None, ("dp", "tp")),
        P("ep", None, ("dp", "tp")),
        P("ep", None, ("dp", "tp")),
    )
    out_specs = (P(("dp", "ep"), "tp", None), P(("dp", "tp", "ep"), None))
    return jax.shard_map(
        per_device, mesh=mesh, in_specs=in_specs, out_specs=out_specs, check_vma=False
    )
```
